128 devices in a mesh: dom: 16 (over z, x), grp: 8 (over y, core).
Axes of the slice: x: 4, y: 4, z: 4, core: 2. Of those that a mesh axis runs over, the one named last changes fastest.
Arguments:
- nodes: bfloat16 [131072, 256], P(('dom', 'grp')), may hold values from -6 to 6
- edges: bfloat16 [524288, 256], P(('dom', 'grp')), may hold values from -6 to 6
- senders: int32 [524288], P(('dom', 'grp')), may hold values from 0 to 1535, as said below
- receivers: int32 [524288], P(('dom', 'grp')), may hold values from 0 to 1023, as said below
- edge_count: int32 [128], P(('dom', 'grp')), may hold values from 64 to 512, as said below
- halo_rows: int32 [128, 16, 32], P(('dom', 'grp')), may hold values from 0 to 1023, as said below
- aggregates: int32 [131072], P(('dom', 'grp')), may hold values from 0 to 1023, as said below
- coarse_edges: bfloat16 [16, 4096, 256], P('dom'), may hold values from -6 to 6
- coarse_senders: int32 [16, 4096], P('dom'), may hold values from 0 to 1023
- coarse_receivers: int32 [16, 4096], P('dom'), may hold values from 0 to 127
- cotangent: bfloat16 [131072, 256], P(('dom', 'grp')), may hold values from -6 to 6
- fine_weights: bfloat16 [1792, 256], replicated, may hold values from -0.21875 to 0.21875
- coarse_weights: bfloat16 [1792, 256], replicated, may hold values from -0.21875 to 0.21875
Outputs:
- fine_out: bfloat16 [131072, 256], P(('dom', 'grp'))
- node_grad: bfloat16 [131072, 256], P(('dom', 'grp'))
- edge_grad: bfloat16 [524288, 256], P(('dom', 'grp'))
- fine_weight_grad: float32 [1792, 256], replicated
- coarse_weight_grad: float32 [1792, 256], replicated
The draws below stay inside these ranges and needn't reach their ends.
Inputs may be any that keep to these rules, and one draw needn't show every extreme that they name: `senders`: A value at least 1024 names a halo slot from a partition at another dom index with the same grp index. The receivers of edge slots 512 * t to 512 * t + 511 of a partition lie in its node rows 128 * t to 128 * t + 127. `edge_count`: each count is 512 divided by a power of two; some partition has 512 and some 64. `halo_rows`: entry [q, p, t] is a local node row of partition q; the rows of one list are distinct. `aggregates`: every coarse node of a group is the aggregate of exactly 8 fine nodes of that group.
All inputs are finite; a program needn't handle non-finite values.
Results may differ from the reference program's by a relative error of at most 0.035.
Values may be sent and summed in bfloat16 or wider, within the bound.
A program may use at most 128 MiB of HBM per device.

```python
import jax
import jax.numpy as jnp
from jax import lax

LATENT = 256
NODE_DEV = 1024
SLOT = 32
NODES = 131072
EDGES = 524288
COARSE = 16384
COARSE_EDGES = 65536
N_DOM = 16
N_GRP = 8


def pair_counts(key):
    seeded = jax.random.fold_in(key, 101)
    counts = jax.random.randint(jax.random.fold_in(seeded, 1), (N_DOM, N_GRP, N_DOM), 1, SLOT + 1)
    domain = jnp.arange(N_DOM, dtype=jnp.int32)
    chosen = (domain[:, None] + 1 + jax.random.randint(jax.random.fold_in(seeded, 2), (N_DOM, N_GRP), 0, N_DOM - 1)) % N_DOM
    counts = jnp.where(domain[None, None, :] == chosen[:, :, None], SLOT, counts)
    counts = jnp.where(domain[None, None, :] == domain[:, None, None], 0, counts)
    return counts.at[N_DOM - 1, 0, 0].set(SLOT)


def draw_senders(key, part):
    counts = pair_counts(key)
    key = jax.random.fold_in(key, 3)
    edge_ids = jnp.arange(EDGES, dtype=jnp.int32)
    holder = edge_ids // (4 * NODE_DEV)
    home_dom = holder // N_GRP
    home_group = holder % N_GRP
    remote = jax.random.randint(jax.random.fold_in(key, 1), (EDGES,), 0, 3) == 0
    nearby = jax.random.randint(jax.random.fold_in(key, 2), (EDGES,), 0, NODE_DEV)
    partner = (home_dom + 1 + jax.random.randint(jax.random.fold_in(key, 4), (EDGES,), 0, N_DOM - 1)) % N_DOM
    filled = counts[partner, home_group, home_dom]
    slot_pick = jax.random.randint(jax.random.fold_in(key, 5), (EDGES,), 0, filled)
    picked = jnp.where(remote, NODE_DEV + partner * SLOT + slot_pick, nearby).astype(jnp.int32)
    return picked.at[0].set(NODE_DEV + N_DOM * SLOT - 1).at[1].set(0).astype(jnp.int32)


def draw_receivers(key, part):
    key = jax.random.fold_in(key, 7)
    edge_ids = jnp.arange(EDGES, dtype=jnp.int32)
    tile_index = edge_ids % (4 * NODE_DEV) // 512
    return (tile_index * 128 + jax.random.randint(key, (EDGES,), 0, 128)).astype(jnp.int32)


def draw_edge_count(key, part):
    key = jax.random.fold_in(key, 9)
    devices = N_DOM * N_GRP
    halving = jax.random.randint(jax.random.fold_in(key, 1), (devices,), 0, 4)
    busiest = jax.random.randint(jax.random.fold_in(key, 2), (), 0, devices)
    lightest = (busiest + 1 + jax.random.randint(jax.random.fold_in(key, 3), (), 0, devices - 1)) % devices
    device_ids = jnp.arange(devices, dtype=jnp.int32)
    halving = jnp.where(device_ids == busiest, 0, jnp.where(device_ids == lightest, 3, halving))
    return jnp.right_shift(jnp.full((devices,), 512, jnp.int32), halving).astype(jnp.int32)


def draw_halo_rows(key, part):
    key = jax.random.fold_in(key, 13)
    devices = N_DOM * N_GRP
    scores = jax.random.randint(key, (devices, N_DOM, NODE_DEV), 0, 2 ** 20) * NODE_DEV + jnp.arange(NODE_DEV, dtype=jnp.int32)
    scores = scores.at[0, 0, NODE_DEV - 1].set(-2).at[0, 0, 0].set(-1)
    ranked = jnp.argsort(scores, axis=-1)
    return ranked[:, :, :SLOT].astype(jnp.int32)


def draw_aggregates(key, part):
    key = jax.random.fold_in(key, 17)
    subkeys = jax.random.split(key, N_DOM)

    def shuffle_group(subkey):
        return jax.random.permutation(subkey, N_GRP * NODE_DEV)
    shuffles = jax.vmap(shuffle_group)(subkeys)
    return (shuffles // 8).reshape(-1).astype(jnp.int32)


def draw_coarse_senders(key, part):
    key = jax.random.fold_in(key, 19)
    picked = jax.random.randint(key, (N_DOM, N_GRP * NODE_DEV // 2), 0, N_GRP * (NODE_DEV // 8)).astype(jnp.int32)
    return picked.at[0, 0].set(0).at[0, 1].set(N_GRP * (NODE_DEV // 8) - 1).astype(jnp.int32)


def draw_coarse_receivers(key, part):
    key = jax.random.fold_in(key, 23)
    picked = jax.random.randint(key, (N_DOM, N_GRP * NODE_DEV // 2), 0, NODE_DEV // 8).astype(jnp.int32)
    return picked.at[0, 0].set(0).at[0, 1].set(NODE_DEV // 8 - 1).astype(jnp.int32)


def shard_levels(rng, dims, cuts, low, largest):
    def one(dim, shards_of):
        heights = jax.random.uniform(jax.random.fold_in(jax.random.fold_in(rng, 6), dim), (shards_of,), jnp.float32, low / len(cuts), largest / len(cuts))
        return jnp.repeat(jnp.exp(heights), dims[dim] // shards_of).reshape((-1,) + (1,) * (len(dims) - dim - 1))

    level = one(*cuts[0])
    for cut in cuts[1:]:
        level = level * one(*cut)
    return level


def noise(own_key, extent, scale, limit, shards=(), kind=jnp.bfloat16):
    values = scale * jax.random.normal(own_key, extent, jnp.float32)
    if shards:
        values = values * shard_levels(own_key, extent, shards, -0.22, 0.18)
    return jnp.clip(values, -limit, limit).astype(kind)


def setup_inputs(seed: int = 0) -> dict:
    key_of = jax.random.split(jax.random.key(seed), 14)
    return {
        "nodes": noise(key_of[0], (NODES, LATENT), 1.0, 6.0, ((0, 128),)),
        "edges": noise(key_of[1], (EDGES, LATENT), 1.0, 6.0, ((0, 128),)),
        "senders": draw_senders(jax.random.fold_in(key_of[13], 71), 0),
        "receivers": draw_receivers(jax.random.fold_in(key_of[13], 71), 0),
        "edge_count": draw_edge_count(jax.random.fold_in(key_of[13], 71), 0),
        "halo_rows": draw_halo_rows(jax.random.fold_in(key_of[13], 71), 0),
        "aggregates": draw_aggregates(jax.random.fold_in(key_of[13], 71), 0),
        "coarse_edges": noise(key_of[7], (N_DOM, N_GRP * NODE_DEV // 2, LATENT), 1.0, 6.0, ((0, 16),)),
        "coarse_senders": draw_coarse_senders(jax.random.fold_in(key_of[13], 71), 0),
        "coarse_receivers": draw_coarse_receivers(jax.random.fold_in(key_of[13], 71), 0),
        "cotangent": noise(key_of[10], (NODES, LATENT), 1.0, 6.0, ((0, 128),)),
        "fine_weights": noise(key_of[11], (7 * LATENT, LATENT), (3 * LATENT) ** -0.5, 0.21875),
        "coarse_weights": noise(key_of[12], (7 * LATENT, LATENT), (3 * LATENT) ** -0.5, 0.21875),
    }


def stored(values):
    return lax.optimization_barrier(values.astype(jnp.bfloat16))

def layer_norm(values):
    centre = values - lax.optimization_barrier(jnp.mean(values, axis=-1, keepdims=True))
    spread = lax.optimization_barrier(jnp.mean(centre * centre, axis=-1, keepdims=True))
    return centre * lax.rsqrt(spread + 1e-05)

def two_layer(inputs, first, second):
    hidden = jnp.dot(inputs, first, preferred_element_type=jnp.float32)
    active = jax.nn.silu(hidden).astype(jnp.bfloat16)
    return layer_norm(jnp.dot(active, second, preferred_element_type=jnp.float32))

def edge_message(edge_rows, sender_rows, target_rows, weights):
    feat_width = edge_rows.shape[1]
    narrow = weights.astype(jnp.bfloat16)
    joined = jnp.concatenate([edge_rows, sender_rows, target_rows], axis=1)
    return stored(two_layer(joined, narrow[:3 * feat_width], narrow[3 * feat_width:4 * feat_width]))

def node_update(node_rows, summed, weights):
    feat_width = node_rows.shape[1]
    narrow = weights.astype(jnp.bfloat16)
    joined = jnp.concatenate([node_rows, summed], axis=1)
    change = two_layer(joined, narrow[4 * feat_width:6 * feat_width], narrow[6 * feat_width:])
    return stored(node_rows.astype(jnp.float32) + change)

def reference(nodes, edges, senders, receivers, edge_count, halo_rows, aggregates, coarse_edges, coarse_senders, coarse_receivers, cotangent, fine_weights, coarse_weights):
    devices = N_DOM * N_GRP
    per_dev = 4 * NODE_DEV
    own_rows = NODE_DEV // 8
    group_rows = own_rows * N_GRP
    per_block = coarse_senders.shape[1] // N_GRP
    edge_ids = jnp.arange(EDGES, dtype=jnp.int32)
    holder = edge_ids // per_dev
    home_dom = holder // N_GRP
    home_group = holder % N_GRP
    offset = jnp.maximum(senders - NODE_DEV, 0)
    source = offset // SLOT * N_GRP + home_group
    far_row = halo_rows[source, home_dom, offset % SLOT]
    global_send = jnp.where(senders < NODE_DEV, holder * NODE_DEV + senders, source * NODE_DEV + far_row).astype(jnp.int32)
    global_recv = (holder * NODE_DEV + receivers).astype(jnp.int32)
    live_mask = edge_ids % per_dev % 512 < edge_count[holder]
    node_ids = jnp.arange(NODES, dtype=jnp.int32)
    coarse_of = (node_ids // (N_GRP * NODE_DEV) * group_rows + aggregates).astype(jnp.int32)
    coarse_ids = jnp.arange(COARSE_EDGES, dtype=jnp.int32)
    coarse_group = coarse_ids // (N_GRP * per_block)
    coarse_send = (coarse_group * group_rows + coarse_senders.reshape(-1)).astype(jnp.int32)
    coarse_recv = (coarse_group * group_rows + coarse_ids // per_block % N_GRP * own_rows + coarse_receivers.reshape(-1)).astype(jnp.int32)
    flat_coarse = coarse_edges.reshape(COARSE_EDGES, LATENT)

    def forward(node_values, edge_values, fine_float, coarse_float):
        node_wide = node_values.astype(jnp.float32)

        def edge_block(pieces):
            edge_rows, send_rows, recv_rows, recv_local, live_rows = pieces
            messages = edge_message(edge_rows, jnp.take(node_wide, send_rows, axis=0).astype(jnp.bfloat16), jnp.take(node_wide, recv_rows, axis=0).astype(jnp.bfloat16), fine_float)
            kept = jnp.where(live_rows[:, None], messages.astype(jnp.float32), 0.0)
            return jax.ops.segment_sum(kept, recv_local, num_segments=NODE_DEV).astype(jnp.bfloat16)
        summed = lax.map(jax.checkpoint(edge_block), (edge_values.reshape(devices, per_dev, LATENT), global_send.reshape(devices, per_dev), global_recv.reshape(devices, per_dev), receivers.reshape(devices, per_dev), live_mask.reshape(devices, per_dev)))
        refined = node_update(node_wide.astype(jnp.bfloat16), summed.reshape(NODES, LATENT), fine_float)
        refined_wide = refined.astype(jnp.float32)
        coarse_input = stored(jax.ops.segment_sum(refined_wide, coarse_of, num_segments=COARSE) * 0.125)
        coarse_wide = coarse_input.astype(jnp.float32)
        coarse_messages = edge_message(flat_coarse, jnp.take(coarse_wide, coarse_send, axis=0).astype(jnp.bfloat16), jnp.take(coarse_wide, coarse_recv, axis=0).astype(jnp.bfloat16), coarse_float)
        coarse_summed = jax.ops.segment_sum(coarse_messages.astype(jnp.float32), coarse_recv, num_segments=COARSE).astype(jnp.bfloat16)
        coarse_output = node_update(coarse_wide.astype(jnp.bfloat16), coarse_summed, coarse_float)
        lifted = jnp.take(coarse_output.astype(jnp.float32), coarse_of, axis=0)
        return (refined_wide + lifted).astype(jnp.bfloat16)
    fine_out, backward = jax.vjp(forward, nodes, edges, fine_weights.astype(jnp.float32), coarse_weights.astype(jnp.float32))
    node_grad, edge_grad, fine_grad, coarse_grad = backward(cotangent)
    return (fine_out, node_grad, edge_grad, fine_grad * EDGES ** (-0.5), coarse_grad * COARSE_EDGES ** (-0.5))
```

```python
import jax
import jax.numpy as jnp
from jax import lax
from jax.experimental import pallas as pl
from jax.experimental.pallas import tpu as pltpu
from jax.sharding import PartitionSpec as P

MESH = pl.DeviceIdType.MESH
BF = jnp.bfloat16
F32 = jnp.float32
W = 256
DOM = 16
GRP = 8
TILES = 8
FINE_SCALE = 524288 ** (-0.5)
COARSE_SCALE = 65536 ** (-0.5)


def mm(a, b):
    return jnp.dot(a, b, preferred_element_type=F32)


def mm_nt(a, b):
    return lax.dot_general(a, b, (((1,), (1,)), ((), ())), preferred_element_type=F32)


def mm_tn(a, b):
    return lax.dot_general(a, b, (((0,), (0,)), ((), ())), preferred_element_type=F32)


def iota(shape, axis):
    return lax.broadcasted_iota(jnp.int32, shape, axis)


def hot(mask):
    return jnp.where(mask, 1.0, 0.0).astype(BF)


def column(row):
    return jnp.broadcast_to(row, (128, 128)).T


def silu_parts(h):
    sig = 1.0 / (1.0 + jnp.exp(-h))
    active = h * sig
    return active.astype(BF), (sig * (1.0 + h - active)).astype(BF)


def norm(z):
    centre = z - jnp.mean(z, axis=-1, keepdims=True)
    rs = lax.rsqrt(jnp.mean(centre * centre, axis=-1, keepdims=True) + 1e-05)
    return centre * rs, rs


def norm_back(dy, y, rs):
    first = jnp.mean(dy, axis=-1, keepdims=True)
    second = jnp.mean(dy * y, axis=-1, keepdims=True)
    return (rs * (dy - first - y * second)).astype(BF)


class Exchange:
    def __init__(self, axis, count, me, src, dst, ssem, rsem, off):
        self.axis, self.count, self.me = axis, count, me
        self.src, self.dst, self.ssem, self.rsem, self.off = src, dst, ssem, rsem, off

    def copy(self, k):
        peer = lax.rem(self.me + k, self.count)
        return pltpu.make_async_remote_copy(
            src_ref=self.src(peer),
            dst_ref=self.dst(k),
            send_sem=self.ssem.at[self.off + k],
            recv_sem=self.rsem.at[self.off + k],
            device_id={self.axis: peer},
            device_id_type=MESH,
        )

    def each(self, act):
        def step(k, carry):
            act(self.copy(k))
            return carry

        lax.fori_loop(1, self.count, step, 0)

    def start(self):
        self.each(lambda c: c.start())

    def wait_recv(self):
        self.each(lambda c: c.wait_recv())

    def wait_send(self):
        self.each(lambda c: c.wait_send())


def summed_blocks(own, received, count):
    total = own.astype(F32)
    for k in range(1, count):
        total = total + received[k].astype(F32)
    return total


class AllReduce:
    def __init__(self, refs, d, g, ssem, rsem):
        (self.sa, self.ra, self.ta, self.ua, self.va, self.oa,
         self.sb, self.rb, self.tb, self.ub, self.vb, self.ob) = refs
        self.d, self.g = d, g
        mk = lambda axis, src, dst, off: Exchange(
            axis, DOM if axis == "dom" else GRP, d if axis == "dom" else g, src, dst, ssem, rsem, off)
        sa, ra, ta, ua, va, oa = self.sa, self.ra, self.ta, self.ua, self.va, self.oa
        sb, rb, tb, ub, vb, ob = self.sb, self.rb, self.tb, self.ub, self.vb, self.ob
        self.a1 = mk("grp", lambda p: sa.at[p], lambda k: ra.at[k], 0)
        self.b1 = mk("dom", lambda p: sb.at[p], lambda k: rb.at[k], 8)
        self.a2 = mk("dom", lambda p: ta.at[p], lambda k: ua.at[k], 24)
        self.b2 = mk("grp", lambda p: tb.at[p], lambda k: ub.at[k], 40)
        self.a3 = mk("dom", lambda p: va.at[d], lambda k: va.at[d], 48)
        self.b3 = mk("grp", lambda p: vb.at[g], lambda k: vb.at[g], 64)
        self.a4 = mk("grp", lambda p: oa.at[g], lambda k: oa.at[g], 72)
        self.b4 = mk("dom", lambda p: ob.at[d], lambda k: ob.at[d], 80)

    def stage1(self):
        self.b1.start()
        self.a1.start()

    def stage2(self):
        self.a1.wait_recv()
        total = summed_blocks(self.sa[self.g], self.ra, GRP)
        step = total.shape[0] // 8
        for p in range(DOM):
            i, j = p // 2, p % 2
            self.ta[p] = total[i * step:(i + 1) * step, j * 128:(j + 1) * 128]
        self.a2.start()
        self.b1.wait_recv()
        total = summed_blocks(self.sb[self.d], self.rb, DOM)
        step = total.shape[0] // 4
        for p in range(GRP):
            i, j = p // 2, p % 2
            self.tb[p] = total[i * step:(i + 1) * step, j * 128:(j + 1) * 128]
        self.b2.start()

    def stage3(self):
        self.a2.wait_recv()
        self.va[self.d] = summed_blocks(self.ta[self.d], self.ua, DOM)
        self.a3.start()
        self.b2.wait_recv()
        self.vb[self.g] = summed_blocks(self.tb[self.g], self.ub, GRP)
        self.b3.start()

    def stage4(self):
        self.b3.wait_recv()
        step = self.vb.shape[1]
        for p in range(GRP):
            i, j = p // 2, p % 2
            self.ob[self.d, i * step:(i + 1) * step, j * 128:(j + 1) * 128] = self.vb[p].astype(BF)
        self.b4.start()
        self.a3.wait_recv()
        step = self.va.shape[1]
        for p in range(DOM):
            i, j = p // 2, p % 2
            self.oa[self.g, i * step:(i + 1) * step, j * 128:(j + 1) * 128] = self.va[p].astype(BF)
        self.a4.start()

    def finish(self):
        self.a4.wait_recv()
        self.b4.wait_recv()

    def drain(self):
        for e in (self.a1, self.b1, self.a2, self.b2, self.a3, self.b3, self.a4, self.b4):
            e.wait_send()


def reduce_scratch(rows_a, rows_b):
    ra, rb = rows_a // 8, rows_b // 16
    return [
        pltpu.VMEM((8, ra, W), BF), pltpu.VMEM((8, ra, W), BF),
        pltpu.VMEM((16, ra // 8, 128), F32), pltpu.VMEM((16, ra // 8, 128), F32),
        pltpu.VMEM((16, ra // 8, 128), F32), pltpu.VMEM((8, ra, W), BF),
        pltpu.VMEM((16, rb, W), BF), pltpu.VMEM((16, rb, W), BF),
        pltpu.VMEM((8, rb // 4, 128), F32), pltpu.VMEM((8, rb // 4, 128), F32),
        pltpu.VMEM((8, rb // 4, 128), F32), pltpu.VMEM((16, rb, W), BF),
    ]


def kernel(
    nodes, edges, snd, rcv, cnt, halo, agg, cedges, csnd, crcv, cot, fw, cw,
    fine_out, node_grad, edge_grad, fwg, cwg, *s
):
    (hpad, hr, ohh, outg, hin, m_t, m_n, cps, cpr, wcat, p_r, xcat, act, gpr, yv, rsv, summed,
     an, gn, yn, rsn, refined, rsb, rsr, cinb, ce, cx, cwc, cact, cgp, cy, crs, coutb,
     ssb, ssr, dcinb, rg, dnp, dsm, s_s, s_r, g_ae, g_b, hret, hrin, ssem, rsem, csem,
     arc_s, arc_r, are_s, are_r) = s[:52]
    arc_refs, are_refs = s[52:64], s[64:76]
    d = lax.axis_index("dom")
    g = lax.axis_index("grp")
    count = cnt[0]

    ce_copy = pltpu.make_async_copy(cedges.at[0, pl.ds(pl.multiple_of(g * 512, 512), 512)], ce, csem)
    ce_copy.start()
    barrier = pltpu.get_barrier_semaphore()

    def greet_dom(k, c):
        pl.semaphore_signal(barrier, inc=1, device_id={"dom": lax.rem(d + k, DOM)}, device_id_type=MESH)
        return c

    def greet_grp(k, c):
        pl.semaphore_signal(barrier, inc=1, device_id={"grp": lax.rem(g + k, GRP)}, device_id_type=MESH)
        return c

    lax.fori_loop(1, DOM, greet_dom, 0)
    lax.fori_loop(1, GRP, greet_grp, 0)

    x_halo = Exchange("dom", DOM, d, lambda p: outg.at[p], lambda k: hin.at[d], ssem, rsem, 0)
    x_ret = Exchange("dom", DOM, d, lambda p: hret.at[p], lambda k: hrin.at[d], ssem, rsem, 16)
    x_cp = Exchange("grp", GRP, g, lambda p: cps.at[p], lambda k: cpr.at[k], ssem, rsem, 32)
    x_rs = Exchange("grp", GRP, g, lambda p: rsb.at[p], lambda k: rsr.at[k], ssem, rsem, 40)
    x_cin = Exchange("grp", GRP, g, lambda p: cinb.at[g], lambda k: cinb.at[g], ssem, rsem, 48)
    x_cout = Exchange("grp", GRP, g, lambda p: coutb.at[g], lambda k: coutb.at[g], ssem, rsem, 56)
    x_ss = Exchange("grp", GRP, g, lambda p: ssb.at[p], lambda k: ssr.at[k], ssem, rsem, 64)
    x_dcin = Exchange("grp", GRP, g, lambda p: dcinb.at[g], lambda k: dcinb.at[g], ssem, rsem, 72)
    arc = AllReduce(arc_refs, d, g, arc_s, arc_r)
    are = AllReduce(are_refs, d, g, are_s, are_r)

    lane = iota((128, 128), 1)
    sub = iota((128, 128), 0)

    hpad[...] = jnp.zeros_like(hpad)
    hpad[:, 0:32] = halo[...]
    padded = hpad[...]
    rolled = [padded] + [pltpu.roll(padded, 32 * i, 1) for i in range(1, 4)]
    for j in range(4):
        row = rolled[0][4 * j:4 * j + 1]
        for i in range(1, 4):
            row = row + rolled[i][4 * j + i:4 * j + i + 1]
        hr[j:j + 1, :] = row
        col = column(row)
        for b in range(8):
            ohh[128 * j:128 * j + 128, 128 * b:128 * b + 128] = hot(col == lane + 128 * b)
    outg[...] = mm(ohh[...], nodes[...]).astype(BF).reshape(16, 32, W)
    hin[d] = jnp.zeros((32, W), BF)
    pl.semaphore_wait(barrier, DOM + GRP - 2)
    x_halo.start()

    def member(j, c):
        row = agg[pl.ds(j, 1), :]
        col = column(row)
        at = pl.multiple_of(j * 128, 128)
        for b in range(8):
            m_t[128 * b:128 * b + 128, pl.ds(at, 128)] = hot(sub + 128 * b == row)
            m_n[pl.ds(at, 128), 128 * b:128 * b + 128] = hot(col == lane + 128 * b)
        return c

    lax.fori_loop(0, 8, member, 0)
    cps[...] = mm(m_t[...], cot[...]).astype(BF).reshape(8, 128, W)
    x_cp.start()

    wcat[0:256] = fw[0:256]
    wcat[256:1280] = mm(nodes[...], fw[256:512]).astype(BF)
    p_r[...] = mm(nodes[...], fw[512:768]).astype(BF)
    x_halo.wait_recv()
    wcat[1280:1792] = mm(hin[...].reshape(512, W), fw[256:512]).astype(BF)

    def edge_forward(t, c):
        base = pl.multiple_of(t * 512, 512)
        nbase = pl.multiple_of(t * 128, 128)
        xcat[:, 0:256] = edges[pl.ds(base, 512), :]
        back = []
        for j in range(4):
            srow = snd[pl.ds(4 * t + j, 1), :]
            rrow = rcv[pl.ds(4 * t + j, 1), :] - 128 * t
            scol = column(srow)
            rcol = column(rrow)
            for b in range(12):
                xcat[128 * j:128 * j + 128, 256 + 128 * b:384 + 128 * b] = hot(scol == lane + 128 * b)
            xcat[128 * j:128 * j + 128, 1792:1920] = hot((rcol == lane) & (sub + 128 * j < count))
            back.append(hot((rrow == sub) & (lane + 128 * j < count)))
        wcat[1792:1920] = p_r[pl.ds(nbase, 128), :]
        h = mm(xcat[...], wcat[...])
        a, gp = silu_parts(h)
        act[pl.ds(base, 512), :] = a
        gpr[pl.ds(base, 512), :] = gp
        y, rs = norm(mm(a, fw[768:1024]))
        y = y.astype(BF)
        yv[pl.ds(base, 512), :] = y
        rsv[pl.ds(base, 512), :] = rs
        summed[pl.ds(nbase, 128), :] = mm(jnp.concatenate(back, axis=1), y).astype(BF)
        return c

    lax.fori_loop(0, TILES, edge_forward, 0)

    def node_forward(t, c):
        rows = pl.ds(pl.multiple_of(t * 512, 512), 512)
        h = mm(nodes[rows, :], fw[1024:1280]) + mm(summed[rows, :], fw[1280:1536])
        a, gp = silu_parts(h)
        an[rows, :] = a
        gn[rows, :] = gp
        y, rs = norm(mm(a, fw[1536:1792]))
        yn[rows, :] = y.astype(BF)
        rsn[rows, :] = rs
        refined[rows, :] = (nodes[rows, :].astype(F32) + y).astype(BF)
        return c

    lax.fori_loop(0, 2, node_forward, 0)

    def restrict(k, c):
        p = lax.rem(g + k, GRP)
        part = mm(m_t[pl.ds(pl.multiple_of(p * 128, 128), 128), :], refined[...]) * 0.125
        rsb[p] = part.astype(BF)

        @pl.when(k < GRP)
        def _():
            x_rs.copy(k).start()

        return c

    lax.fori_loop(1, GRP + 1, restrict, 0)
    x_rs.wait_recv()
    cin = summed_blocks(rsb[g], rsr, GRP).astype(BF)
    cinb[g] = cin
    x_cin.start()

    ce_copy.wait()
    cx[:, 0:256] = ce[...]
    cback = []
    for j in range(4):
        srow = csnd[pl.ds(4 * g + j, 1), :]
        rrow = crcv[pl.ds(4 * g + j, 1), :]
        scol = column(srow)
        rcol = column(rrow)
        for b in range(8):
            cx[128 * j:128 * j + 128, 256 + 128 * b:384 + 128 * b] = hot(scol == lane + 128 * b)
        cx[128 * j:128 * j + 128, 1280:1408] = hot(rcol == lane)
        cback.append(hot(rrow == sub))
    cback = jnp.concatenate(cback, axis=1)
    cwc[0:256] = cw[0:256]
    cwc[1280:1408] = mm(cin, cw[512:768]).astype(BF)
    x_cp.wait_recv()
    pg = summed_blocks(cps[g], cpr, GRP).astype(BF).astype(F32)
    x_cin.wait_recv()
    cwc[256:1280] = mm(cinb[...].reshape(1024, W), cw[256:512]).astype(BF)
    ca, cg = silu_parts(mm(cx[...], cwc[...]))
    cact[...] = ca
    cgp[...] = cg
    y, rs = norm(mm(ca, cw[768:1024]))
    y = y.astype(BF)
    cy[...] = y
    crs[...] = rs
    csum = mm(cback, y).astype(BF)
    cna, cng = silu_parts(mm(cin, cw[1024:1280]) + mm(csum, cw[1280:1536]))
    cny, cnrs = norm(mm(cna, cw[1536:1792]))
    coutb[g] = (cin.astype(F32) + cny).astype(BF)
    x_cout.start()

    cndz = norm_back(pg, cny, cnrs)
    cndh = (mm_nt(cndz, cw[1536:1792]) * cng.astype(F32)).astype(BF)
    dcin_part = pg + mm_nt(cndh, cw[1024:1280])
    dcsum = mm_nt(cndh, cw[1280:1536]).astype(BF)
    cdz = norm_back(mm(cx[:, 1280:1408], dcsum), cy[...].astype(F32), crs[...])
    cdh = (mm_nt(cdz, cw[768:1024]) * cgp[...].astype(F32)).astype(BF)
    gp = cgp
    gp[...] = cdh

    def sender_sum(k, c):
        p = lax.rem(g + k, GRP)
        rows = [hot(csnd[pl.ds(4 * g + j, 1), :] - 128 * p == sub) for j in range(4)]
        ssb[p] = mm(jnp.concatenate(rows, axis=1), gp[...]).astype(BF)

        @pl.when(k < GRP)
        def _():
            x_ss.copy(k).start()

        return c

    lax.fori_loop(1, GRP + 1, sender_sum, 0)
    s_cr = mm(cback, cdh).astype(BF)

    def put_a(at, value):
        value = value.astype(BF)
        for b in range(2):
            arc.sa[at // 128 + b] = value[128 * b:128 * b + 128]

    def put_b(at, value):
        value = value.astype(BF)
        pos = 0
        while pos < 256:
            block, inside = (at + pos) // 96, (at + pos) % 96
            n = min(96 - inside, 256 - pos)
            arc.sb[block, inside:inside + n, :] = value[pos:pos + n]
            pos += n

    put_a(0, mm_tn(ce[...], cdh))
    put_a(768, mm_tn(cact[...], cdz))
    put_b(0, mm_tn(cin, cndh))
    put_b(256, mm_tn(csum, cndh))
    put_b(512, mm_tn(cna, cndz))
    dcin_part = dcin_part + mm_nt(s_cr, cw[512:768])
    x_ss.wait_recv()
    s_tot = summed_blocks(ssb[g], ssr, GRP).astype(BF)
    dcinb[g] = (dcin_part + mm_nt(s_tot, cw[256:512])).astype(BF)
    x_dcin.start()
    put_a(256, mm_tn(cin, s_tot))
    put_a(512, mm_tn(cin, s_cr))

    x_cout.wait_recv()
    fine_out[...] = (refined[...].astype(F32) + mm(m_n[...], coutb[...].reshape(1024, W))).astype(BF)
    x_dcin.wait_recv()
    rg[...] = (cot[...].astype(F32) + 0.125 * mm(m_n[...], dcinb[...].reshape(1024, W))).astype(BF)

    dz = norm_back(rg[...].astype(F32), yn[...].astype(F32), rsn[...])
    dh = (mm_nt(dz, fw[1536:1792]) * gn[...].astype(F32)).astype(BF)
    dnp[...] = rg[...].astype(F32) + mm_nt(dh, fw[1024:1280])
    dsm[...] = mm_nt(dh, fw[1280:1536]).astype(BF)
    put_b(768, mm_tn(nodes[...], dh))
    put_b(1024, mm_tn(summed[...], dh))
    put_b(1280, mm_tn(an[...], dz))
    arc.stage1()

    s_s[...] = jnp.zeros_like(s_s)
    g_ae[...] = jnp.zeros_like(g_ae)
    g_b[...] = jnp.zeros_like(g_b)

    def edge_backward(t, c):
        base = pl.multiple_of(t * 512, 512)
        nbase = pl.multiple_of(t * 128, 128)
        cols, back, srows = [], [], []
        for j in range(4):
            rrow = rcv[pl.ds(4 * t + j, 1), :] - 128 * t
            cols.append(hot((column(rrow) == lane) & (sub + 128 * j < count)))
            back.append(hot((rrow == sub) & (lane + 128 * j < count)))
            srows.append(snd[pl.ds(4 * t + j, 1), :])
        dmsg = mm(jnp.concatenate(cols, axis=0), dsm[pl.ds(nbase, 128), :])
        dz = norm_back(dmsg, yv[pl.ds(base, 512), :].astype(F32), rsv[pl.ds(base, 512), :])
        dh = (mm_nt(dz, fw[768:1024]) * gpr[pl.ds(base, 512), :].astype(F32)).astype(BF)
        edge_grad[pl.ds(base, 512), :] = mm_nt(dh, fw[0:256]).astype(BF)
        g_b[...] += mm_tn(act[pl.ds(base, 512), :], dz)
        g_ae[...] += mm_tn(edges[pl.ds(base, 512), :], dh)
        s_r[pl.ds(nbase, 128), :] = mm(jnp.concatenate(back, axis=1), dh).astype(BF)
        for b in range(12):
            block = jnp.concatenate([hot(srow - 128 * b == sub) for srow in srows], axis=1)
            s_s[128 * b:128 * b + 128, :] += mm(block, dh)
        return c

    lax.fori_loop(0, TILES // 2, edge_backward, 0)
    arc.stage2()
    lax.fori_loop(TILES // 2, TILES, edge_backward, 0)

    ss = s_s[...].astype(BF)
    hret[...] = mm_nt(ss[1024:1536], fw[256:512]).astype(BF).reshape(16, 32, W)
    x_ret.start()
    for b in range(4):
        are.sa[b] = g_ae[64 * b:64 * b + 64].astype(BF)
    g_as = (mm_tn(nodes[...], ss[0:1024]) + mm_tn(hin[...].reshape(512, W), ss[1024:1536])).astype(BF)
    for b in range(4):
        are.sa[4 + b] = g_as[64 * b:64 * b + 64]
    g_ar = mm_tn(nodes[...], s_r[...]).astype(BF)
    for b in range(8):
        are.sb[b] = g_ar[32 * b:32 * b + 32]
        are.sb[8 + b] = g_b[32 * b:32 * b + 32].astype(BF)
    are.stage1()
    arc.stage3()
    own = dnp[...] + mm_nt(ss[0:1024], fw[256:512]) + mm_nt(s_r[...], fw[512:768])
    hrin[d] = jnp.zeros((32, W), BF)
    x_ret.wait_recv()
    node_grad[...] = (own + mm_tn(ohh[...], hrin[...].reshape(512, W))).astype(BF)
    are.stage2()
    arc.stage4()
    are.stage3()
    are.stage4()
    arc.finish()
    cwg[0:1024] = arc.oa[...].reshape(1024, W).astype(F32) * COARSE_SCALE
    cwg[1024:1792] = arc.ob[0:8].reshape(768, W).astype(F32) * COARSE_SCALE
    fwg[1024:1792] = arc.ob[8:16].reshape(768, W).astype(F32) * FINE_SCALE
    are.finish()
    fwg[0:512] = are.oa[...].reshape(512, W).astype(F32) * FINE_SCALE
    fwg[512:1024] = are.ob[...].reshape(512, W).astype(F32) * FINE_SCALE

    for x in (x_halo, x_ret, x_cp, x_rs, x_cin, x_cout, x_ss, x_dcin):
        x.wait_send()
    arc.drain()
    are.drain()


def body(
    nodes, edges, senders, receivers, edge_count, halo_rows, aggregates,
    coarse_edges, coarse_senders, coarse_receivers, cotangent, fine_weights, coarse_weights,
):
    vm = pl.BlockSpec(memory_space=pltpu.VMEM)
    V = pltpu.VMEM
    scratch = [
        V((16, 128), jnp.int32),
        V((8, 128), jnp.int32),
        V((512, 1024), BF),
        V((16, 32, W), BF),
        V((16, 32, W), BF),
        V((1024, 1024), BF),
        V((1024, 1024), BF),
        V((8, 128, W), BF),
        V((8, 128, W), BF),
        V((1920, W), BF),
        V((1024, W), BF),
        V((512, 1920), BF),
        V((4096, W), BF),
        V((4096, W), BF),
        V((4096, W), BF),
        V((4096, 1), F32),
        V((1024, W), BF),
        V((1024, W), BF),
        V((1024, W), BF),
        V((1024, W), BF),
        V((1024, 1), F32),
        V((1024, W), BF),
        V((8, 128, W), BF),
        V((8, 128, W), BF),
        V((8, 128, W), BF),
        V((512, W), BF),
        V((512, 1408), BF),
        V((1408, W), BF),
        V((512, W), BF),
        V((512, W), BF),
        V((512, W), BF),
        V((512, 1), F32),
        V((8, 128, W), BF),
        V((8, 128, W), BF),
        V((8, 128, W), BF),
        V((8, 128, W), BF),
        V((1024, W), BF),
        V((1024, W), F32),
        V((1024, W), BF),
        V((1536, W), F32),
        V((1024, W), BF),
        V((256, W), F32),
        V((256, W), F32),
        V((16, 32, W), BF),
        V((16, 32, W), BF),
        pltpu.SemaphoreType.DMA((80,)),
        pltpu.SemaphoreType.DMA((80,)),
        pltpu.SemaphoreType.DMA,
        pltpu.SemaphoreType.DMA((96,)),
        pltpu.SemaphoreType.DMA((96,)),
        pltpu.SemaphoreType.DMA((96,)),
        pltpu.SemaphoreType.DMA((96,)),
    ] + reduce_scratch(1024, 1536) + reduce_scratch(512, 512)
    return pl.pallas_call(
        kernel,
        out_shape=(
            jax.ShapeDtypeStruct((1024, W), BF),
            jax.ShapeDtypeStruct((1024, W), BF),
            jax.ShapeDtypeStruct((4096, W), BF),
            jax.ShapeDtypeStruct((1792, W), F32),
            jax.ShapeDtypeStruct((1792, W), F32),
        ),
        in_specs=[vm, vm, vm, vm, pl.BlockSpec(memory_space=pltpu.SMEM), vm, vm,
                  pl.BlockSpec(memory_space=pl.ANY), vm, vm, vm, vm, vm],
        out_specs=(vm,) * 5,
        scratch_shapes=scratch,
        compiler_params=pltpu.CompilerParams(
            collective_id=0, has_side_effects=True, vmem_limit_bytes=60 * 1024 * 1024
        ),
    )(
        nodes, edges, senders.reshape(32, 128), receivers.reshape(32, 128), edge_count,
        halo_rows.reshape(16, 32), aggregates.reshape(8, 128), coarse_edges,
        coarse_senders.reshape(32, 128), coarse_receivers.reshape(32, 128), cotangent,
        fine_weights, coarse_weights,
    )


def solution(mesh):
    both = ("dom", "grp")
    placed = (
        P(both, None), P(both, None), P(both), P(both), P(both), P(both, None, None), P(both),
        P("dom", None, None), P("dom", None), P("dom", None), P(both, None), P(), P(),
    )
    return jax.shard_map(
        body, mesh=mesh, in_specs=placed,
        out_specs=(P(both, None), P(both, None), P(both, None), P(), P()),
        check_vma=False,
    )
```

```python
import jax
import jax.numpy as jnp
from jax import lax
from jax.experimental import pallas as pl
from jax.experimental.pallas import tpu as pltpu
from jax.sharding import PartitionSpec as P

MESH = pl.DeviceIdType.MESH
BF = jnp.bfloat16
F32 = jnp.float32
W = 256
DOM = 16
GRP = 8
TILES = 8
YS = 4
FINE_SCALE = 524288 ** (-0.5)
COARSE_SCALE = 65536 ** (-0.5)


def mm(a, b):
    return jnp.dot(a, b, preferred_element_type=F32)


def mm_nt(a, b):
    return lax.dot_general(a, b, (((1,), (1,)), ((), ())), preferred_element_type=F32)


def mm_tn(a, b):
    return lax.dot_general(a, b, (((0,), (0,)), ((), ())), preferred_element_type=F32)


def iota(shape, axis):
    return lax.broadcasted_iota(jnp.int32, shape, axis)


def hot(mask):
    return jnp.where(mask, 1.0, 0.0).astype(BF)


def column(row):
    return jnp.broadcast_to(row, (128, 128)).T


def silu_parts(h):
    sig = 1.0 / (1.0 + jnp.exp(-h))
    active = h * sig
    return active.astype(BF), (sig * (1.0 + h - active)).astype(BF)


def norm(z):
    centre = z - jnp.mean(z, axis=-1, keepdims=True)
    rs = lax.rsqrt(jnp.mean(centre * centre, axis=-1, keepdims=True) + 1e-05)
    return centre * rs, rs


def norm_back(dy, y, rs):
    first = jnp.mean(dy, axis=-1, keepdims=True)
    second = jnp.mean(dy * y, axis=-1, keepdims=True)
    return (rs * (dy - first - y * second)).astype(BF)


class Links:
    def __init__(self, ssem, rsem):
        self.d, self.g = lax.axis_index("dom"), lax.axis_index("grp")
        self.y, self.core = self.g // 2, lax.rem(self.g, 2)
        self.ssem, self.rsem, self.used = ssem, rsem, 0
        self.all = []

    def exchange(self, kind, src, dst):
        x = Exchange(self, kind, src, dst, self.used)
        self.used += x.count
        self.all.append(x)
        return x


class Exchange:
    def __init__(self, at, kind, src, dst, off):
        self.at, self.kind, self.src, self.dst, self.off = at, kind, src, dst, off
        self.count = {"dom": DOM, "grp": GRP, "y": YS, "mate": 2}[kind]

    def copy(self, k):
        at = self.at
        if self.kind == "dom":
            p = lax.rem(at.d + k, DOM)
            device = {"dom": p}
        elif self.kind == "grp":
            p = lax.rem(at.g + k, GRP)
            device = {"grp": p}
        elif self.kind == "y":
            p = lax.rem(at.y + k, YS)
            device = {"grp": 2 * p + at.core}
        else:
            p = 1 - at.core
            device = {"grp": 2 * at.y + p}
        return pltpu.make_async_remote_copy(
            src_ref=self.src(p),
            dst_ref=self.dst(k),
            send_sem=self.at.ssem.at[self.off + k],
            recv_sem=self.at.rsem.at[self.off + k],
            device_id=device,
            device_id_type=MESH,
        )

    def each(self, act):
        def step(k, carry):
            act(self.copy(k))
            return carry

        if self.count <= YS:
            for k in range(1, self.count):
                step(k, 0)
        else:
            lax.fori_loop(1, self.count, step, 0)

    def start(self):
        self.each(lambda c: c.start())

    def wait_recv(self):
        self.each(lambda c: c.wait_recv())

    def wait_send(self):
        self.each(lambda c: c.wait_send())


def total_of(first, blocks, which):
    total = first.astype(F32)
    for k in which:
        total = total + blocks[k].astype(F32)
    return total


class GroupSum:
    def __init__(self, links, s, m, t, r):
        self.links, self.s, self.m, self.t, self.r = links, s, m, t, r
        self.first = links.exchange("mate", lambda p: s.at[p], lambda k: m)
        self.second = links.exchange("y", lambda p: t.at[p], lambda k: r.at[k])

    def pair(self):
        self.first.wait_recv()
        self.t[...] = (self.s[self.links.core].astype(F32) + self.m[...].astype(F32)).astype(BF)
        self.second.start()

    def result(self):
        self.second.wait_recv()
        return total_of(self.t[self.links.y], self.r, range(1, YS))


class GroupGather:
    def __init__(self, links, b):
        self.links, self.b = links, b
        g, y, core = links.g, links.y, links.core
        self.mate = links.exchange("mate", lambda p: b.at[g], lambda k: b.at[g])
        self.far = links.exchange("y", lambda p: b.at[g], lambda k: b.at[g])
        self.passed = []
        for k in range(1, YS):
            p = 2 * lax.rem(y + YS - k, YS) + core
            self.passed.append(links.exchange("mate", lambda q, p=p: b.at[p], lambda q, p=p: b.at[p]))

    def start(self):
        self.far.start()
        self.mate.start()

    def wait_recv(self):
        for k in range(1, YS):
            self.far.copy(k).wait_recv()
            self.passed[k - 1].start()
        self.mate.wait_recv()
        for x in self.passed:
            x.wait_recv()


class EarlySum:
    def __init__(self, links, s, m, t, r, v, o):
        self.links, self.s, self.m, self.t, self.r, self.v, self.o = links, s, m, t, r, v, o
        d, y, core = links.d, links.y, links.core
        self.x0 = links.exchange("mate", lambda p: s.at[p], lambda k: m)
        self.x1 = links.exchange("dom", lambda p: t.at[p], lambda k: r.at[k])
        self.x2 = links.exchange("y", lambda p: v.at[y], lambda k: v.at[y])
        self.x3 = links.exchange("dom", lambda p: o.at[core, d], lambda k: o.at[core, d])
        self.x4 = links.exchange("mate", lambda p: o.at[core], lambda k: o.at[core])

    def stage0(self):
        self.x0.start()

    def stage1(self):
        self.x0.wait_recv()
        self.t[...] = (self.s[self.links.core].astype(F32) + self.m[...].astype(F32)).astype(BF)
        self.x1.start()

    def stage2(self):
        self.x1.wait_recv()
        self.v[self.links.y] = total_of(self.t[self.links.d], self.r, range(1, DOM)).astype(BF)
        self.x2.start()

    def stage3(self):
        self.x2.wait_recv()
        self.o[self.links.core, self.links.d] = total_of(self.v[0], self.v, range(1, YS)).astype(BF)
        self.x3.start()

    def stage4(self):
        self.x3.wait_recv()
        self.x4.start()

    def finish(self):
        self.x4.wait_recv()


class LateSum:
    def __init__(self, links, sa, ra, va, oa, sb, rb, vb, ob):
        self.links = links
        self.sa, self.ra, self.va, self.oa = sa, ra, va, oa
        self.sb, self.rb, self.vb, self.ob = sb, rb, vb, ob
        d, g = links.d, links.g
        self.a1 = links.exchange("grp", lambda p: sa.at[p], lambda k: ra.at[k])
        self.b1 = links.exchange("dom", lambda p: sb.at[p], lambda k: rb.at[k])
        self.a2 = links.exchange("dom", lambda p: va.at[d], lambda k: va.at[d])
        self.b2 = links.exchange("grp", lambda p: vb.at[g], lambda k: vb.at[g])
        self.a3 = links.exchange("grp", lambda p: oa.at[g], lambda k: oa.at[g])
        self.b3 = links.exchange("dom", lambda p: ob.at[d], lambda k: ob.at[d])

    def stage2(self):
        d, g = self.links.d, self.links.g
        self.a1.wait_recv()
        self.va[d] = total_of(self.sa[g], self.ra, range(1, GRP)).astype(BF)
        self.a2.start()
        self.b1.wait_recv()
        self.vb[g] = total_of(self.sb[d], self.rb, range(1, DOM)).astype(BF)
        self.b2.start()

    def stage3(self):
        d, g = self.links.d, self.links.g
        self.b2.wait_recv()
        self.ob[d] = total_of(self.vb[0], self.vb, range(1, GRP)).astype(BF)
        self.b3.start()
        self.a2.wait_recv()
        self.oa[g] = total_of(self.va[0], self.va, range(1, DOM)).astype(BF)
        self.a3.start()

    def finish(self):
        self.a3.wait_recv()
        self.b3.wait_recv()


def put(ref, lead, at, value):
    value = value.astype(BF)
    rows, pos = ref.shape[-2], 0
    while pos < value.shape[0]:
        block, inside = (at + pos) // rows, (at + pos) % rows
        n = min(rows - inside, value.shape[0] - pos)
        ref[lead(block) + (slice(inside, inside + n), slice(None))] = value[pos:pos + n]
        pos += n


def halves(block):
    return (block // DOM, block % DOM)


def single(block):
    return (block,)


def kernel(
    nodes_h, edges_h, snd, rcv, cnt, halo, agg, cedges_h, csnd, crcv, cot_h, fw_h, cw_h,
    fine_out_h, node_grad_h, edge_grad_h, grads_h, *s
):
    (nodes, edges, cot, fw, cw, ce, fine_out, node_grad,
     hpad, hr, ohh, outg, hin, m_t, m_n, oh, wcat, p_r, act, gpr, yv, rsv, summed,
     an, gn, yn, rsn, refined, cinb, cx, cwc, cact, cgp, cy, crs, coutb,
     dcinb, rg, dnp, dsm, s_s, s_r, g_ae, g_b, hret, hrin, ssem, rsem, isem, osem) = s[:50]
    rest = list(s[50:])
    edge_grad, staged = yv, act

    def take(n):
        out = rest[:n]
        del rest[:n]
        return out

    links = Links(ssem, rsem)
    d, g, y, core = links.d, links.g, links.y, links.core
    count = cnt[0]

    loads = [
        pltpu.make_async_copy(src, dst, isem.at[i])
        for i, (src, dst) in enumerate((
            (nodes_h, nodes), (fw_h, fw), (cot_h, cot), (edges_h, edges), (cw_h, cw),
            (cedges_h.at[0, pl.ds(pl.multiple_of(g * 512, 512), 512)], ce),
        ))
    ]
    for c in loads:
        c.start()
    ld_nodes, ld_fw, ld_cot, ld_edges, ld_cw, ld_ce = loads
    barrier = pltpu.get_barrier_semaphore()

    def greet_dom(k, c):
        pl.semaphore_signal(barrier, inc=1, device_id={"dom": lax.rem(d + k, DOM)}, device_id_type=MESH)
        return c

    def greet_grp(k, c):
        pl.semaphore_signal(barrier, inc=1, device_id={"grp": lax.rem(g + k, GRP)}, device_id_type=MESH)
        return c

    lax.fori_loop(1, DOM, greet_dom, 0)
    lax.fori_loop(1, GRP, greet_grp, 0)

    x_halo = links.exchange("dom", lambda p: outg.at[p], lambda k: hin.at[d])
    x_ret = links.exchange("dom", lambda p: hret.at[p], lambda k: hrin.at[d])
    pro = GroupSum(links, *take(4))
    res = GroupSum(links, *take(4))
    sen = GroupSum(links, *take(4))
    x_cin = GroupGather(links, cinb)
    x_cout = GroupGather(links, coutb)
    x_dcin = GroupGather(links, dcinb)
    early = EarlySum(links, *take(6))
    middle = EarlySum(links, *take(6))
    late = LateSum(links, *take(8))

    lane = iota((128, 128), 1)
    sub = iota((128, 128), 0)

    hpad[...] = jnp.zeros_like(hpad)
    hpad[:, 0:32] = halo[...]
    padded = hpad[...]
    rolled = [padded] + [pltpu.roll(padded, 32 * i, 1) for i in range(1, 4)]
    for j in range(4):
        row = rolled[0][4 * j:4 * j + 1]
        for i in range(1, 4):
            row = row + rolled[i][4 * j + i:4 * j + i + 1]
        hr[j:j + 1, :] = row
        col = column(row)
        for b in range(8):
            ohh[128 * j:128 * j + 128, 128 * b:128 * b + 128] = hot(col == lane + 128 * b)
    hin[d] = jnp.zeros((32, W), BF)
    hrin[d] = jnp.zeros((32, W), BF)
    ld_nodes.wait()
    outg[...] = mm(ohh[...], nodes[...]).astype(BF).reshape(16, 32, W)
    pl.semaphore_wait(barrier, DOM + GRP - 2)
    x_halo.start()

    def member(j, c):
        row = agg[pl.ds(j, 1), :]
        col = column(row)
        at = pl.multiple_of(j * 128, 128)
        for b in range(8):
            m_t[b % 2, 128 * (b // 2):128 * (b // 2) + 128, pl.ds(at, 128)] = hot(sub + 128 * b == row)
            m_n[pl.ds(at, 128), 128 * b:128 * b + 128] = hot(col == lane + 128 * b)
        return c

    lax.fori_loop(0, 8, member, 0)
    ld_cot.wait()
    for h in range(2):
        pro.s[h] = mm(m_t[h], cot[...]).astype(BF).reshape(YS, 128, W)
    pro.first.start()

    ld_fw.wait()
    wcat[0:256] = fw[0:256]
    wcat[256:1280] = mm(nodes[...], fw[256:512]).astype(BF)
    p_r[...] = mm(nodes[...], fw[512:768]).astype(BF)

    def edge_hot(t, c):
        for j in range(4):
            rows = slice(128 * j, 128 * j + 128)
            scol = column(snd[pl.ds(4 * t + j, 1), :])
            rcol = column(rcv[pl.ds(4 * t + j, 1), :] - 128 * t)
            for b in range(12):
                oh[t, b, rows, :] = hot(scol == lane + 128 * b)
            oh[t, 12, rows, :] = hot((rcol == lane) & (sub + 128 * j < count))
        return c

    lax.fori_loop(0, TILES, edge_hot, 0)
    pro.pair()
    ld_edges.wait()
    x_halo.wait_recv()
    wcat[1280:1792] = mm(hin[...].reshape(512, W), fw[256:512]).astype(BF)

    def edge_forward(t, c):
        base = pl.multiple_of(t * 512, 512)
        nbase = pl.multiple_of(t * 128, 128)
        back = []
        for j in range(4):
            rrow = rcv[pl.ds(4 * t + j, 1), :] - 128 * t
            back.append(hot((rrow == sub) & (lane + 128 * j < count)))
        wcat[1792:1920] = p_r[pl.ds(nbase, 128), :]
        joined = jnp.concatenate([edges[pl.ds(base, 512), :]] + [oh[t, b] for b in range(13)], axis=1)
        h = mm(joined, wcat[...])
        a, gp = silu_parts(h)
        act[pl.ds(base, 512), :] = a
        gpr[pl.ds(base, 512), :] = gp
        y, rs = norm(mm(a, fw[768:1024]))
        y = y.astype(BF)
        yv[pl.ds(base, 512), :] = y
        rsv[pl.ds(base, 512), :] = rs
        summed[pl.ds(nbase, 128), :] = mm(jnp.concatenate(back, axis=1), y).astype(BF)
        return c

    lax.fori_loop(0, TILES, edge_forward, 0)

    def node_forward(t, c):
        rows = pl.ds(pl.multiple_of(t * 512, 512), 512)
        h = mm(nodes[rows, :], fw[1024:1280]) + mm(summed[rows, :], fw[1280:1536])
        a, gp = silu_parts(h)
        an[rows, :] = a
        gn[rows, :] = gp
        y, rs = norm(mm(a, fw[1536:1792]))
        yn[rows, :] = y.astype(BF)
        rsn[rows, :] = rs
        refined[rows, :] = (nodes[rows, :].astype(F32) + y).astype(BF)
        return c

    lax.fori_loop(0, 2, node_forward, 0)

    res.s[1 - core] = (mm(m_t[1 - core], refined[...]) * 0.125).astype(BF).reshape(YS, 128, W)
    res.first.start()
    res.s[core] = (mm(m_t[core], refined[...]) * 0.125).astype(BF).reshape(YS, 128, W)
    res.pair()

    def edge_hot_back(t, c):
        for j in range(4):
            rows = slice(128 * j, 128 * j + 128)
            srow = snd[pl.ds(4 * t + j, 1), :]
            rrow = rcv[pl.ds(4 * t + j, 1), :] - 128 * t
            for b in range(12):
                oh[t, b, rows, :] = hot(srow == sub + 128 * b)
            oh[t, 12, rows, :] = hot((rrow == sub) & (lane + 128 * j < count))
        return c

    ld_ce.wait()
    ld_cw.wait()
    cx[:, 0:256] = ce[...]
    cback = []
    for j in range(4):
        srow = csnd[pl.ds(4 * g + j, 1), :]
        rrow = crcv[pl.ds(4 * g + j, 1), :]
        scol = column(srow)
        rcol = column(rrow)
        for b in range(8):
            cx[128 * j:128 * j + 128, 256 + 128 * b:384 + 128 * b] = hot(scol == lane + 128 * b)
        cx[128 * j:128 * j + 128, 1280:1408] = hot(rcol == lane)
        cback.append(hot(rrow == sub))
    cback = jnp.concatenate(cback, axis=1)
    cwc[0:256] = cw[0:256]
    pg = pro.result().astype(BF).astype(F32)
    lax.fori_loop(0, 3, edge_hot_back, 0)
    cin = res.result().astype(BF)
    cinb[g] = cin
    x_cin.start()
    cwc[1280:1408] = mm(cin, cw[512:768]).astype(BF)
    lax.fori_loop(3, TILES, edge_hot_back, 0)
    x_cin.wait_recv()
    cwc[256:1280] = mm(cinb[...].reshape(1024, W), cw[256:512]).astype(BF)
    ca, cg = silu_parts(mm(cx[...], cwc[...]))
    cact[...] = ca
    cgp[...] = cg
    cyn, rs = norm(mm(ca, cw[768:1024]))
    cyn = cyn.astype(BF)
    cy[...] = cyn
    crs[...] = rs
    csum = mm(cback, cyn).astype(BF)
    cna, cng = silu_parts(mm(cin, cw[1024:1280]) + mm(csum, cw[1280:1536]))
    cny, cnrs = norm(mm(cna, cw[1536:1792]))
    coutb[g] = (cin.astype(F32) + cny).astype(BF)

    cndz = norm_back(pg, cny, cnrs)
    cndh = (mm_nt(cndz, cw[1536:1792]) * cng.astype(F32)).astype(BF)
    dcin_part = pg + mm_nt(cndh, cw[1024:1280])
    dcsum = mm_nt(cndh, cw[1280:1536]).astype(BF)
    cdz = norm_back(mm(cx[:, 1280:1408], dcsum), cy[...].astype(F32), crs[...])
    cdh = (mm_nt(cdz, cw[768:1024]) * cgp[...].astype(F32)).astype(BF)

    def sender_sum(half):
        blocks = []
        for p in range(YS):
            at = 128 * (2 * p + half)
            blocks.append(jnp.concatenate(
                [hot(csnd[pl.ds(4 * g + j, 1), :] - at == sub) for j in range(4)], axis=1))
        sen.s[half] = mm(jnp.concatenate(blocks, axis=0), cdh).astype(BF).reshape(YS, 128, W)

    sender_sum(1 - core)
    sen.first.start()
    sender_sum(core)
    s_cr = mm(cback, cdh).astype(BF)
    sen.pair()
    x_cout.start()
    put(early.s, halves, 0, mm_tn(ce[...], cdh))
    put(early.s, halves, 256, mm_tn(cact[...], cdz))
    put(early.s, halves, 512, mm_tn(cin, cndh))
    put(early.s, halves, 768, mm_tn(csum, cndh))
    put(early.s, halves, 1024, mm_tn(cna, cndz))
    put(middle.s, halves, 0, mm_tn(cin, s_cr))
    dcin_part = dcin_part + mm_nt(s_cr, cw[512:768])
    s_tot = sen.result().astype(BF)
    dcinb[g] = (dcin_part + mm_nt(s_tot, cw[256:512])).astype(BF)
    x_dcin.start()
    put(early.s, halves, 1280, mm_tn(cin, s_tot))
    early.stage0()

    x_cout.wait_recv()
    fine_out[...] = (refined[...].astype(F32) + mm(m_n[...], coutb[...].reshape(1024, W))).astype(BF)
    st_fine = pltpu.make_async_copy(fine_out, fine_out_h, osem.at[0])
    st_fine.start()
    early.stage1()
    x_dcin.wait_recv()
    rg[...] = (cot[...].astype(F32) + 0.125 * mm(m_n[...], dcinb[...].reshape(1024, W))).astype(BF)

    dz = norm_back(rg[...].astype(F32), yn[...].astype(F32), rsn[...])
    dh = (mm_nt(dz, fw[1536:1792]) * gn[...].astype(F32)).astype(BF)
    dnp[...] = rg[...].astype(F32) + mm_nt(dh, fw[1024:1280])
    dsm[...] = mm_nt(dh, fw[1280:1536]).astype(BF)
    put(middle.s, halves, 256, mm_tn(nodes[...], dh))
    put(middle.s, halves, 512, mm_tn(summed[...], dh))
    put(middle.s, halves, 768, mm_tn(an[...], dz))
    middle.stage0()
    early.stage2()

    s_s[...] = jnp.zeros_like(s_s)
    g_ae[...] = jnp.zeros_like(g_ae)
    g_b[...] = jnp.zeros_like(g_b)

    def edge_backward(t, c):
        base = pl.multiple_of(t * 512, 512)
        nbase = pl.multiple_of(t * 128, 128)
        cols = []
        for j in range(4):
            rrow = rcv[pl.ds(4 * t + j, 1), :] - 128 * t
            cols.append(hot((column(rrow) == lane) & (sub + 128 * j < count)))

        def turned(b):
            return jnp.concatenate([oh[t, b, 128 * j:128 * j + 128, :] for j in range(4)], axis=1)

        dmsg = mm(jnp.concatenate(cols, axis=0), dsm[pl.ds(nbase, 128), :])
        dz = norm_back(dmsg, yv[pl.ds(base, 512), :].astype(F32), rsv[pl.ds(base, 512), :])
        dh = (mm_nt(dz, fw[768:1024]) * gpr[pl.ds(base, 512), :].astype(F32)).astype(BF)
        gpr[pl.ds(base, 512), :] = dh
        g_b[...] += mm_tn(act[pl.ds(base, 512), :], dz)
        g_ae[...] += mm_tn(edges[pl.ds(base, 512), :], dh)
        for q in range(3):
            part = jnp.concatenate([turned(4 * q + b) for b in range(4)], axis=0)
            s_s[512 * q:512 * q + 512, :] += mm(part, dh)
        s_r[pl.ds(nbase, 128), :] = mm(turned(12), dh).astype(BF)
        return c

    lax.fori_loop(0, 2, edge_backward, 0)
    early.stage3()
    middle.stage1()
    lax.fori_loop(2, TILES, edge_backward, 0)

    put(late.sa, single, 0, g_b[...])
    late.a1.start()
    ss = s_s[...].astype(BF)
    g_as = mm_tn(nodes[...], ss[0:1024]) + mm_tn(hin[...].reshape(512, W), ss[1024:1536])
    put(late.sb, single, 0, g_ae[...])
    put(late.sb, single, 256, g_as)
    put(late.sb, single, 512, mm_tn(nodes[...], s_r[...]))
    late.b1.start()
    hret[...] = mm_nt(ss[1024:1536], fw[256:512]).astype(BF).reshape(16, 32, W)
    x_ret.start()
    middle.stage2()
    early.stage4()

    def edge_out(t, c):
        rows = pl.ds(pl.multiple_of(t * 512, 512), 512)
        edge_grad[rows, :] = mm_nt(gpr[rows, :], fw[0:256]).astype(BF)
        return c

    lax.fori_loop(0, TILES, edge_out, 0)
    st_edge = pltpu.make_async_copy(edge_grad, edge_grad_h, osem.at[1])
    st_edge.start()
    late.stage2()
    middle.stage3()
    own = dnp[...] + mm_nt(ss[0:1024], fw[256:512]) + mm_nt(s_r[...], fw[512:768])
    x_ret.wait_recv()
    node_grad[...] = (own + mm_tn(ohh[...], hrin[...].reshape(512, W))).astype(BF)
    st_node = pltpu.make_async_copy(node_grad, node_grad_h, osem.at[2])
    st_node.start()
    late.stage3()
    middle.stage4()
    early.finish()
    stores = [st_fine, st_edge, st_node]

    def store(ref, at):
        rows = ref.shape[0]
        copy = pltpu.make_async_copy(ref, grads_h.at[pl.ds(at, rows)], osem.at[len(stores)])
        copy.start()
        stores.append(copy)

    def store_blocks(ref, at):
        rows = ref.shape[-2]
        if len(ref.shape) == 4:
            for h in range(2):
                store_blocks(ref.at[h], at + h * DOM * rows)
        else:
            n = ref.shape[0]
            flat = staged.at[pl.ds(at, n * rows)]
            flat[...] = ref[...].reshape(n * rows, W)
            store(flat, at)

    store_blocks(early.o, 0)
    middle.finish()
    store_blocks(middle.o, 1536)
    late.finish()
    store_blocks(late.oa, 2560)
    store_blocks(late.ob, 2816)
    for c in stores:
        c.wait()
    for x in links.all:
        x.wait_send()


def place(
    fine_h, node_h, edge_h, grads_h, fine_o, node_o, edge_o, fw_o, cw_o,
    fine, node, edge, grads, fwg, cwg, lsem, ssem,
):
    half = edge.shape[0] // 2
    parts = [(grads_h, grads, None), (fine_h, fine, fine_o), (node_h, node, node_o)]
    for i in range(2):
        rows = pl.ds(half * i, half)
        parts.append((edge_h.at[rows], edge.at[rows], edge_o.at[rows]))
    loads = [pltpu.make_async_copy(a, b, lsem.at[i]) for i, (a, b, c) in enumerate(parts)]
    moves = [pltpu.make_async_copy(b, c, ssem.at[i]) for i, (a, b, c) in enumerate(parts) if i > 0]
    for c in loads:
        c.start()
    for c, m in zip(loads[1:], moves):
        c.wait()
        m.start()
    loads[0].wait()

    def scaled(at, rows, scale):
        return grads[at:at + rows].astype(F32) * scale

    cwg[0:256] = scaled(0, 256, COARSE_SCALE)
    cwg[256:768] = scaled(1280, 512, COARSE_SCALE)
    cwg[768:1792] = scaled(256, 1024, COARSE_SCALE)
    fwg[0:768] = scaled(2816, 768, FINE_SCALE)
    fwg[768:1024] = scaled(2560, 256, FINE_SCALE)
    fwg[1024:1792] = scaled(1792, 768, FINE_SCALE)
    last = [pltpu.make_async_copy(fwg, fw_o, ssem.at[5]), pltpu.make_async_copy(cwg, cw_o, ssem.at[6])]
    for c in last:
        c.start()
    for c in moves + last:
        c.wait()


def body(
    nodes, edges, senders, receivers, edge_count, halo_rows, aggregates,
    coarse_edges, coarse_senders, coarse_receivers, cotangent, fine_weights, coarse_weights,
):
    vm = pl.BlockSpec(memory_space=pltpu.VMEM)
    hbm = pl.BlockSpec(memory_space=pl.ANY)
    V = pltpu.VMEM
    scratch = [
        V((1024, W), BF),
        V((4096, W), BF),
        V((1024, W), BF),
        V((1792, W), BF),
        V((1792, W), BF),
        V((512, W), BF),
        V((1024, W), BF),
        V((1024, W), BF),
        V((16, 128), jnp.int32),
        V((8, 128), jnp.int32),
        V((512, 1024), BF),
        V((16, 32, W), BF),
        V((16, 32, W), BF),
        V((2, 512, 1024), BF),
        V((1024, 1024), BF),
        V((8, 13, 512, 128), BF),
        V((1920, W), BF),
        V((1024, W), BF),
        V((4096, W), BF),
        V((4096, W), BF),
        V((4096, W), BF),
        V((4096, 1), F32),
        V((1024, W), BF),
        V((1024, W), BF),
        V((1024, W), BF),
        V((1024, W), BF),
        V((1024, 1), F32),
        V((1024, W), BF),
        V((8, 128, W), BF),
        V((512, 1408), BF),
        V((1408, W), BF),
        V((512, W), BF),
        V((512, W), BF),
        V((512, W), BF),
        V((512, 1), F32),
        V((8, 128, W), BF),
        V((8, 128, W), BF),
        V((1024, W), BF),
        V((1024, W), F32),
        V((1024, W), BF),
        V((1536, W), F32),
        V((1024, W), BF),
        V((256, W), F32),
        V((256, W), F32),
        V((16, 32, W), BF),
        V((16, 32, W), BF),
        pltpu.SemaphoreType.DMA((256,)),
        pltpu.SemaphoreType.DMA((256,)),
        pltpu.SemaphoreType.DMA((6,)),
        pltpu.SemaphoreType.DMA((12,)),
    ]
    for _ in range(3):
        scratch += [V((2, YS, 128, W), BF), V((YS, 128, W), BF), V((YS, 128, W), BF), V((YS, 128, W), BF)]
    for rows in (48, 32):
        scratch += [V((2, DOM, rows, W), BF), V((DOM, rows, W), BF), V((DOM, rows, W), BF),
                    V((DOM, rows, W), BF), V((YS, rows, W), BF), V((2, DOM, rows, W), BF)]
    scratch += [V((GRP, 32, W), BF), V((GRP, 32, W), BF), V((DOM, 32, W), BF), V((GRP, 32, W), BF),
                V((DOM, 48, W), BF), V((DOM, 48, W), BF), V((GRP, 48, W), BF), V((DOM, 48, W), BF)]
    shape = jax.ShapeDtypeStruct
    fine_out, node_grad, edge_grad, grads = pl.pallas_call(
        kernel,
        out_shape=(shape((1024, W), BF), shape((1024, W), BF), shape((4096, W), BF), shape((3584, W), BF)),
        in_specs=[hbm, hbm, vm, vm, pl.BlockSpec(memory_space=pltpu.SMEM), vm, vm,
                  hbm, vm, vm, hbm, hbm, hbm],
        out_specs=(hbm,) * 4,
        scratch_shapes=scratch,
        compiler_params=pltpu.CompilerParams(
            collective_id=0, has_side_effects=True, vmem_limit_bytes=62 * 1024 * 1024
        ),
    )(
        nodes, edges, senders.reshape(32, 128), receivers.reshape(32, 128), edge_count,
        halo_rows.reshape(16, 32), aggregates.reshape(8, 128), coarse_edges,
        coarse_senders.reshape(32, 128), coarse_receivers.reshape(32, 128), cotangent,
        fine_weights, coarse_weights,
    )
    return pl.pallas_call(
        place,
        out_shape=(shape((1024, W), BF), shape((1024, W), BF), shape((4096, W), BF),
                   shape((1792, W), F32), shape((1792, W), F32)),
        in_specs=[hbm] * 4,
        out_specs=(hbm,) * 5,
        scratch_shapes=[V((1024, W), BF), V((1024, W), BF), V((4096, W), BF), V((3584, W), BF), V((1792, W), F32),
                        V((1792, W), F32), pltpu.SemaphoreType.DMA((5,)), pltpu.SemaphoreType.DMA((7,))],
        compiler_params=pltpu.CompilerParams(vmem_limit_bytes=62 * 1024 * 1024),
    )(fine_out, node_grad, edge_grad, grads)


def solution(mesh):
    both = ("dom", "grp")
    placed = (
        P(both, None), P(both, None), P(both), P(both), P(both), P(both, None, None), P(both),
        P("dom", None, None), P("dom", None), P("dom", None), P(both, None), P(), P(),
    )
    return jax.shard_map(
        body, mesh=mesh, in_specs=placed,
        out_specs=(P(both, None), P(both, None), P(both, None), P(), P()),
        check_vma=False,
    )
```

```python
import jax
import jax.numpy as jnp
from jax import lax
from jax.experimental import pallas as pl
from jax.experimental.pallas import tpu as pltpu
from jax.sharding import PartitionSpec as P

MESH = pl.DeviceIdType.MESH
BF = jnp.bfloat16
F32 = jnp.float32
W = 256
DOM = 16
GRP = 8
TILES = 8
YS = 4
BIG = 2048
FINE_SCALE = 524288 ** (-0.5)
COARSE_SCALE = 65536 ** (-0.5)


def mm(a, b):
    return jnp.dot(a, b, preferred_element_type=F32)


def mm_nt(a, b):
    return lax.dot_general(a, b, (((1,), (1,)), ((), ())), preferred_element_type=F32)


def mm_tn(a, b):
    return lax.dot_general(a, b, (((0,), (0,)), ((), ())), preferred_element_type=F32)


def iota(shape, axis):
    return lax.broadcasted_iota(jnp.int32, shape, axis)


def hot(mask):
    return jnp.where(mask, 1.0, 0.0).astype(BF)


def hot16(mask):
    return jnp.where(mask, jnp.ones(mask.shape, BF), jnp.zeros(mask.shape, BF))


def column(row):
    return jnp.broadcast_to(row, (128, 128)).T


def silu_parts(h):
    sig = 1.0 / (1.0 + jnp.exp(-h))
    active = h * sig
    return active.astype(BF), (sig * (1.0 + h - active)).astype(BF)


def norm(z):
    centre = z - jnp.mean(z, axis=-1, keepdims=True)
    rs = lax.rsqrt(jnp.mean(centre * centre, axis=-1, keepdims=True) + 1e-05)
    return centre * rs, rs


def norm_back(dy, y, rs):
    first = jnp.mean(dy, axis=-1, keepdims=True)
    second = jnp.mean(dy * y, axis=-1, keepdims=True)
    return (rs * (dy - first - y * second)).astype(BF)


def norm_back_centred(dy, y, rs):
    second = jnp.mean(dy * y, axis=-1, keepdims=True)
    return (rs * (dy - y * second)).astype(BF)


def turn(ref, rows, count):
    def step(i, c):
        block = pl.ds(pl.multiple_of(rows + 256 * i, 256), 256)
        ref[block, :] = ref[block, :].T
        return c

    lax.fori_loop(0, count, step, 0)


def mm_turned(ref, rows, count, b):
    left = [ref[rows + 256 * i:rows + 256 * i + 256, :] for i in range(count)]
    return mm(jnp.concatenate(left, axis=1), b)


class Links:
    def __init__(self, ssem, rsem):
        self.d, self.g = lax.axis_index("dom"), lax.axis_index("grp")
        self.y, self.core = self.g // 2, lax.rem(self.g, 2)
        self.ssem, self.rsem, self.used = ssem, rsem, 0
        self.all = []

    def exchange(self, kind, src, dst):
        x = Exchange(self, kind, src, dst, self.used)
        self.used += x.count
        self.all.append(x)
        return x


class Exchange:
    def __init__(self, at, kind, src, dst, off):
        self.at, self.kind, self.src, self.dst, self.off = at, kind, src, dst, off
        self.count = {"dom": DOM, "grp": GRP, "y": YS, "mate": 2}[kind]

    def copy(self, k):
        at = self.at
        if self.kind == "dom":
            p = lax.rem(at.d + k, DOM)
            device = {"dom": p}
        elif self.kind == "grp":
            p = lax.rem(at.g + k, GRP)
            device = {"grp": p}
        elif self.kind == "y":
            p = lax.rem(at.y + k, YS)
            device = {"grp": 2 * p + at.core}
        else:
            p = 1 - at.core
            device = {"grp": 2 * at.y + p}
        return pltpu.make_async_remote_copy(
            src_ref=self.src(p),
            dst_ref=self.dst(k),
            send_sem=self.at.ssem.at[self.off + k],
            recv_sem=self.at.rsem.at[self.off + k],
            device_id=device,
            device_id_type=MESH,
        )

    def each(self, act):
        def step(k, carry):
            act(self.copy(k))
            return carry

        if self.count <= DOM:
            for k in range(1, self.count):
                step(k, 0)
        else:
            lax.fori_loop(1, self.count, step, 0)

    def start(self):
        self.each(lambda c: c.start())

    def wait_recv(self):
        self.each(lambda c: c.wait_recv())

    def wait_send(self):
        self.each(lambda c: c.wait_send())


def total_of(first, blocks, which):
    total = first.astype(F32)
    for k in which:
        total = total + blocks[k].astype(F32)
    return total


class GroupSum:
    def __init__(self, links, s, m, t, r):
        self.links, self.s, self.m, self.t, self.r = links, s, m, t, r
        self.first = links.exchange("mate", lambda p: s.at[p], lambda k: m)
        self.second = links.exchange("y", lambda p: t.at[p], lambda k: r.at[k])

    def pair(self):
        self.first.wait_recv()
        self.t[...] = (self.s[self.links.core].astype(F32) + self.m[...].astype(F32)).astype(BF)
        self.second.start()

    def result(self):
        self.second.wait_recv()
        return total_of(self.t[self.links.y], self.r, range(1, YS))


class GroupGather:
    def __init__(self, links, b):
        self.links, self.b = links, b
        g, y, core = links.g, links.y, links.core
        self.mate = links.exchange("mate", lambda p: b.at[g], lambda k: b.at[g])
        self.far = links.exchange("y", lambda p: b.at[g], lambda k: b.at[g])
        self.passed = []
        for k in range(1, YS):
            p = 2 * lax.rem(y + YS - k, YS) + core
            self.passed.append(links.exchange("mate", lambda q, p=p: b.at[p], lambda q, p=p: b.at[p]))

    def start(self):
        self.far.start()
        self.mate.start()

    def wait_recv(self):
        for k in range(1, YS):
            self.far.copy(k).wait_recv()
            self.passed[k - 1].start()
        self.mate.wait_recv()
        for x in self.passed:
            x.wait_recv()


class AllSum:
    def __init__(self, links, s, m, t, r, v, o):
        self.links, self.s, self.m, self.t, self.r, self.v, self.o = links, s, m, t, r, v, o
        d, y, core = links.d, links.y, links.core
        self.x0 = links.exchange("mate", lambda p: s.at[p], lambda k: m)
        self.x1 = links.exchange("dom", lambda p: t.at[p], lambda k: r.at[k])
        self.x2 = links.exchange("y", lambda p: v.at[y], lambda k: v.at[y])
        self.x3 = links.exchange("dom", lambda p: o.at[core, d], lambda k: o.at[core, d])
        self.x4 = links.exchange("mate", lambda p: o.at[core], lambda k: o.at[core])

    def stage0(self):
        self.x0.start()

    def stage1(self):
        self.x0.wait_recv()
        self.t[...] = (self.s[self.links.core].astype(F32) + self.m[...].astype(F32)).astype(BF)
        self.x1.start()

    def stage2(self):
        self.x1.wait_recv()
        self.v[self.links.y] = total_of(self.t[self.links.d], self.r, range(1, DOM)).astype(BF)
        self.x2.start()

    def stage3(self):
        self.x2.wait_recv()
        self.o[self.links.core, self.links.d] = total_of(self.v[0], self.v, range(1, YS)).astype(BF)
        self.x3.start()

    def stage4(self):
        self.x3.wait_recv()
        self.x4.start()

    def finish(self):
        self.x4.wait_recv()


def put(ref, lead, at, value):
    value = value.astype(BF)
    rows, pos = ref.shape[-2], 0
    while pos < value.shape[0]:
        block, inside = (at + pos) // rows, (at + pos) % rows
        n = min(rows - inside, value.shape[0] - pos)
        ref[lead(block) + (slice(inside, inside + n), slice(None))] = value[pos:pos + n]
        pos += n


def halves(block):
    return (block // DOM, block % DOM)


def kernel(
    nodes_h, edges_h, snd, rcv, cnt, halo, agg, cedges_h, csnd, crcv, cot_h, fw_h, cw_h,
    fine_out_h, node_grad_h, edge_grad_h, grads_h, *s
):
    (nodes, edges, cot, fw, cw, ce,
     hpad, hr, ohh, outg, hin, m_t, oh, ohr, wcat, p_r, act, gpr, yv, rsv, summed,
     an, gn, yn, rsn, refined, cinb, cx, cwc, cact, cgp, cy, crs, coutb,
     dcinb, rg, work, dsm, s_r, hret, hrin, ssem, rsem, isem, osem) = s[:45]
    rest = list(s[45:])
    edge_grad, staged, fine_out, node_grad = yv, act, refined, rg
    s_s, dnp = work.at[0:1536], work.at[1536:2560]
    g_ae, g_b = work.at[2560:2816], work.at[2816:3072]

    def take(n):
        out = rest[:n]
        del rest[:n]
        return out

    links = Links(ssem, rsem)
    d, g, y, core = links.d, links.g, links.y, links.core
    count = cnt[0]

    loads = [
        pltpu.make_async_copy(src, dst, isem.at[i])
        for i, (src, dst) in enumerate((
            (nodes_h, nodes), (fw_h, fw), (cot_h, cot), (edges_h, edges), (cw_h, cw),
            (cedges_h.at[0, pl.ds(pl.multiple_of(g * 512, 512), 512)], ce),
        ))
    ]
    for c in loads:
        c.start()
    ld_nodes, ld_fw, ld_cot, ld_edges, ld_cw, ld_ce = loads
    barrier = pltpu.get_barrier_semaphore()

    def greet_dom(k, c):
        pl.semaphore_signal(barrier, inc=1, device_id={"dom": lax.rem(d + k, DOM)}, device_id_type=MESH)
        return c

    def greet_grp(k, c):
        pl.semaphore_signal(barrier, inc=1, device_id={"grp": lax.rem(g + k, GRP)}, device_id_type=MESH)
        return c

    lax.fori_loop(1, DOM, greet_dom, 0)
    lax.fori_loop(1, GRP, greet_grp, 0)

    x_halo = links.exchange("dom", lambda p: outg.at[p], lambda k: hin.at[d])
    x_ret = links.exchange("dom", lambda p: hret.at[p], lambda k: hrin.at[d])
    pro = GroupSum(links, *take(4))
    res = GroupSum(links, *take(4))
    sen = GroupSum(links, *take(4))
    x_cin = GroupGather(links, cinb)
    x_cout = GroupGather(links, coutb)
    x_dcin = GroupGather(links, dcinb)
    early = AllSum(links, *take(6))
    middle = AllSum(links, *take(6))
    late = AllSum(links, *take(6))

    lane = iota((128, 128), 1)
    sub = iota((128, 128), 0)
    lane16 = lane.astype(jnp.int16)
    sub16 = sub.astype(jnp.int16)

    hpad[...] = jnp.zeros_like(hpad)
    hpad[:, 0:32] = halo[...]
    padded = hpad[...]
    rolled = [padded] + [pltpu.roll(padded, 32 * i, 1) for i in range(1, 4)]
    for j in range(4):
        row = rolled[0][4 * j:4 * j + 1]
        for i in range(1, 4):
            row = row + rolled[i][4 * j + i:4 * j + i + 1]
        hr[j:j + 1, :] = row
        col = column(row)
        for b in range(8):
            ohh[128 * j:128 * j + 128, 128 * b:128 * b + 128] = hot(col == lane + 128 * b)
    hin[d] = jnp.zeros((32, W), BF)
    hrin[d] = jnp.zeros((32, W), BF)
    ld_nodes.wait()
    outg[...] = mm(ohh[...], nodes[...]).astype(BF).reshape(16, 32, W)
    pl.semaphore_wait(barrier, DOM + GRP - 2)
    x_halo.start()

    def member(j, c):
        row = agg[pl.ds(j, 1), :]
        at = pl.multiple_of(j * 128, 128)
        for b in range(8):
            m_t[b % 2, 128 * (b // 2):128 * (b // 2) + 128, pl.ds(at, 128)] = hot(sub + 128 * b == row)
        return c

    lax.fori_loop(0, 8, member, 0)
    ld_cot.wait()
    for h in range(2):
        pro.s[h] = mm(m_t[h], cot[...]).astype(BF).reshape(YS, 128, W)
    pro.first.start()

    ld_fw.wait()
    wcat[0:256] = fw[0:256]
    wcat[256:1280] = mm(nodes[...], fw[256:512]).astype(BF)
    p_r[...] = mm(nodes[...], fw[512:768]).astype(BF)

    def edge_hot(t, c):
        for j in range(4):
            rows = slice(128 * j, 128 * j + 128)
            scol = column(snd[pl.ds(4 * t + j, 1), :]).astype(jnp.int16)
            rcol = column(rcv[pl.ds(4 * t + j, 1), :] - 128 * t)
            for b in range(12):
                oh[t, b, rows, :] = hot16(scol == lane16 + jnp.int16(128 * b))
            ohr[t, rows, :] = hot((rcol == lane) & (sub + 128 * j < count))
        return c

    lax.fori_loop(0, TILES, edge_hot, 0, unroll=2)
    pro.pair()
    ld_edges.wait()

    def edge_local(i, c):
        rows = pl.ds(pl.multiple_of(i * BIG, BIG), BIG)
        tiles = [i * (BIG // 512) + q for q in range(BIG // 512)]
        far = [jnp.concatenate([oh[t, b] for b in range(8)], axis=1) for t in tiles]
        near = [mm(ohr[t], p_r[pl.ds(pl.multiple_of(t * 128, 128), 128), :]) for t in tiles]
        joined = jnp.concatenate([edges[rows, :], jnp.concatenate(far, axis=0)], axis=1)
        work[rows, :] = mm(joined, wcat[0:1280]) + jnp.concatenate(near, axis=0)
        return c

    lax.fori_loop(0, 4096 // BIG, edge_local, 0)
    x_halo.wait_recv()
    wcat[1280:1792] = mm(hin[...].reshape(512, W), fw[256:512]).astype(BF)

    def edge_forward(i, c):
        rows = pl.ds(pl.multiple_of(i * BIG, BIG), BIG)
        tiles = [i * (BIG // 512) + q for q in range(BIG // 512)]
        far = [jnp.concatenate([oh[t, b] for b in range(8, 12)], axis=1) for t in tiles]
        a, gp = silu_parts(work[rows, :] + mm(jnp.concatenate(far, axis=0), wcat[1280:1792]))
        act[rows, :] = a
        gpr[rows, :] = gp
        y, rs = norm(mm(a, fw[768:1024]))
        yv[rows, :] = y.astype(BF)
        rsv[rows, :] = rs
        return c

    def edge_sum(t, c):
        back = []
        for j in range(4):
            rrow = rcv[pl.ds(4 * t + j, 1), :] - 128 * t
            back.append(hot((rrow == sub) & (lane + 128 * j < count)))
        rows = pl.ds(pl.multiple_of(t * 512, 512), 512)
        summed[pl.ds(pl.multiple_of(t * 128, 128), 128), :] = mm(
            jnp.concatenate(back, axis=1), yv[rows, :]).astype(BF)
        return c

    lax.fori_loop(0, 4096 // BIG, edge_forward, 0)
    lax.fori_loop(0, TILES, edge_sum, 0, unroll=TILES)

    a, gp = silu_parts(mm(nodes[...], fw[1024:1280]) + mm(summed[...], fw[1280:1536]))
    an[...] = a
    gn[...] = gp
    ynode, rs = norm(mm(a, fw[1536:1792]))
    yn[...] = ynode.astype(BF)
    rsn[...] = rs
    refined[...] = (nodes[...].astype(F32) + ynode).astype(BF)
    hin_t = p_r
    hin_t[0:512] = hin[...].reshape(512, W)

    res.s[1 - core] = (mm(m_t[1 - core], refined[...]) * 0.125).astype(BF).reshape(YS, 128, W)
    res.first.start()
    res.s[core] = (mm(m_t[core], refined[...]) * 0.125).astype(BF).reshape(YS, 128, W)
    res.pair()

    def edge_hot_back(t, c):
        for j in range(4):
            rows = slice(128 * j, 128 * j + 128)
            srow = jnp.broadcast_to(snd[pl.ds(4 * t + j, 1), :], (128, 128)).astype(jnp.int16)
            rrow = rcv[pl.ds(4 * t + j, 1), :] - 128 * t
            for b in range(12):
                oh[t, b, rows, :] = hot16(srow == sub16 + jnp.int16(128 * b))
            oh[t, 12, rows, :] = hot((rrow == sub) & (lane + 128 * j < count))
        return c

    def member_back(j, c):
        col = column(agg[pl.ds(j, 1), :])
        for b in range(8):
            m_t[j // 4, pl.ds(pl.multiple_of(lax.rem(j, 4) * 128, 128), 128), 128 * b:128 * b + 128] = hot(col == lane + 128 * b)
        return c

    ld_ce.wait()
    ld_cw.wait()
    cback = []
    for j in range(4):
        srow = csnd[pl.ds(4 * g + j, 1), :]
        rrow = crcv[pl.ds(4 * g + j, 1), :]
        scol = column(srow)
        rcol = column(rrow)
        for b in range(8):
            m_t[0, 128 * j:128 * j + 128, 128 * b:128 * b + 128] = hot(scol == lane + 128 * b)
        cx[128 * j:128 * j + 128, :] = hot(rcol == lane)
        cback.append(hot(rrow == sub))
    cback = jnp.concatenate(cback, axis=1)
    cwc[0:256] = cw[0:256]
    pg = pro.result().astype(BF).astype(F32)
    lax.fori_loop(0, 3, edge_hot_back, 0)
    turn(nodes, 0, 4)
    turn(summed, 0, 4)
    turn(an, 0, 4)
    turn(hin_t, 0, 2)
    cin = res.result().astype(BF)
    cinb[g] = cin
    x_cin.start()
    cwc[1280:1408] = mm(cin, cw[512:768]).astype(BF)
    lax.fori_loop(3, TILES, edge_hot_back, 0)
    x_cin.wait_recv()
    cwc[256:1280] = mm(cinb[...].reshape(1024, W), cw[256:512]).astype(BF)
    ca, cg = silu_parts(mm(jnp.concatenate([ce[...], m_t[0], cx[...]], axis=1), cwc[...]))
    cact[...] = ca
    cgp[...] = cg
    cyn, rs = norm(mm(ca, cw[768:1024]))
    cyn = cyn.astype(BF)
    cy[...] = cyn
    crs[...] = rs
    csum = mm(cback, cyn).astype(BF)
    cna, cng = silu_parts(mm(cin, cw[1024:1280]) + mm(csum, cw[1280:1536]))
    cny, cnrs = norm(mm(cna, cw[1536:1792]))
    coutb[g] = (cin.astype(F32) + cny).astype(BF)

    cndz = norm_back(pg, cny, cnrs)
    cndh = (mm_nt(cndz, cw[1536:1792]) * cng.astype(F32)).astype(BF)
    dcin_part = pg + mm_nt(cndh, cw[1024:1280])
    dcsum = mm_nt(cndh, cw[1280:1536]).astype(BF)
    cdz = norm_back(mm(cx[...], dcsum), cy[...].astype(F32), crs[...])
    cdh = (mm_nt(cdz, cw[768:1024]) * cgp[...].astype(F32)).astype(BF)

    def sender_sum(half):
        blocks = []
        for p in range(YS):
            at = 128 * (2 * p + half)
            blocks.append(jnp.concatenate(
                [hot(csnd[pl.ds(4 * g + j, 1), :] - at == sub) for j in range(4)], axis=1))
        sen.s[half] = mm(jnp.concatenate(blocks, axis=0), cdh).astype(BF).reshape(YS, 128, W)

    sender_sum(1 - core)
    sen.first.start()
    sender_sum(core)
    s_cr = mm(cback, cdh).astype(BF)
    sen.pair()
    x_cout.start()
    put(early.s, halves, 0, mm_tn(ce[...], cdh))
    put(early.s, halves, 256, mm_tn(cact[...], cdz))
    put(early.s, halves, 512, mm_tn(cin, cndh))
    put(early.s, halves, 768, mm_tn(csum, cndh))
    put(early.s, halves, 1024, mm_tn(cna, cndz))
    put(middle.s, halves, 0, mm_tn(cin, s_cr))
    dcin_part = dcin_part + mm_nt(s_cr, cw[512:768])
    lax.fori_loop(0, 8, member_back, 0)
    turn(edges, 0, 8)
    s_tot = sen.result().astype(BF)
    dcinb[g] = (dcin_part + mm_nt(s_tot, cw[256:512])).astype(BF)
    x_dcin.start()
    put(early.s, halves, 1280, mm_tn(cin, s_tot))
    early.stage0()

    x_cout.wait_recv()
    fine_out[...] = (refined[...].astype(F32) + mm(m_t[...].reshape(1024, 1024), coutb[...].reshape(1024, W))).astype(BF)
    st_fine = pltpu.make_async_copy(fine_out, fine_out_h, osem.at[0])
    st_fine.start()
    early.stage1()
    turn(edges, 2048, 8)
    turn(act, 0, 16)
    x_dcin.wait_recv()
    rg[...] = (cot[...].astype(F32) + 0.125 * mm(m_t[...].reshape(1024, 1024), dcinb[...].reshape(1024, W))).astype(BF)

    dz = norm_back(rg[...].astype(F32), yn[...].astype(F32), rsn[...])
    dh = (mm_nt(dz, fw[1536:1792]) * gn[...].astype(F32)).astype(BF)
    dnp[...] = rg[...].astype(F32) + mm_nt(dh, fw[1024:1280])
    dsum = mm_nt(dh, fw[1280:1536]).astype(BF).astype(F32)
    dsm[...] = (dsum - jnp.mean(dsum, axis=-1, keepdims=True)).astype(BF)
    put(middle.s, halves, 256, mm_turned(nodes, 0, 4, dh))
    put(middle.s, halves, 512, mm_turned(summed, 0, 4, dh))
    put(middle.s, halves, 768, mm_turned(an, 0, 4, dz))
    middle.stage0()
    early.stage2()

    s_s[...] = jnp.zeros_like(s_s)
    g_ae[...] = jnp.zeros_like(g_ae)
    g_b[...] = jnp.zeros_like(g_b)

    def edge_backward(i):
        base = i * BIG
        rows = pl.ds(base, BIG)
        tiles = [i * (BIG // 512) + q for q in range(BIG // 512)]
        dmsg = jnp.concatenate([mm(ohr[t], dsm[128 * t:128 * t + 128, :]) for t in tiles], axis=0)
        dz = norm_back_centred(dmsg, yv[rows, :].astype(F32), rsv[rows, :])
        dh = (mm_nt(dz, fw[768:1024]) * gpr[rows, :].astype(F32)).astype(BF)
        gpr[rows, :] = dh
        g_b[...] += mm_turned(act, base, BIG // 256, dz)
        g_ae[...] += mm_turned(edges, base, BIG // 256, dh)

        def turned(t, b):
            return jnp.concatenate([oh[t, b, 128 * j:128 * j + 128, :] for j in range(4)], axis=1)

        for q in range(3):
            part = [jnp.concatenate([turned(t, 4 * q + b) for t in tiles], axis=1) for b in range(4)]
            s_s[512 * q:512 * q + 512, :] += mm(jnp.concatenate(part, axis=0), dh)
        for q, t in enumerate(tiles):
            s_r[128 * t:128 * t + 128, :] = mm(turned(t, 12), dh[512 * q:512 * q + 512]).astype(BF)

    for i in range(4096 // BIG):
        if i == 4096 // BIG // 2:
            early.stage3()
            middle.stage1()
        edge_backward(i)

    put(late.s, halves, 0, g_ae[...])
    put(late.s, halves, 256, g_b[...])
    ss = s_s[...].astype(BF)
    put(late.s, halves, 512, mm_turned(nodes, 0, 4, ss[0:1024]) + mm_turned(hin_t, 0, 2, ss[1024:1536]))
    put(late.s, halves, 768, mm_turned(nodes, 0, 4, s_r[...]))
    late.stage0()
    hret[...] = mm_nt(ss[1024:1536], fw[256:512]).astype(BF).reshape(16, 32, W)
    late.stage1()
    x_ret.start()
    middle.stage2()
    early.stage4()

    for i in range(4096 // BIG):
        rows = pl.ds(i * BIG, BIG)
        edge_grad[rows, :] = mm_nt(gpr[rows, :], fw[0:256]).astype(BF)
    st_edge = pltpu.make_async_copy(edge_grad, edge_grad_h, osem.at[1])
    st_edge.start()
    own = dnp[...] + mm_nt(ss[0:1024], fw[256:512]) + mm_nt(s_r[...], fw[512:768])
    late.stage2()
    middle.stage3()
    x_ret.wait_recv()
    node_grad[...] = (own + mm_tn(ohh[...], hrin[...].reshape(512, W))).astype(BF)
    st_node = pltpu.make_async_copy(node_grad, node_grad_h, osem.at[2])
    st_node.start()
    late.stage3()
    early.finish()
    stores = [st_fine, st_edge, st_node]

    def store(ref, at):
        rows = ref.shape[0]
        copy = pltpu.make_async_copy(ref, grads_h.at[pl.ds(at, rows)], osem.at[len(stores)])
        copy.start()
        stores.append(copy)

    def store_blocks(ref, at):
        rows = ref.shape[-2]
        if len(ref.shape) == 4:
            for h in range(2):
                store_blocks(ref.at[h], at + h * DOM * rows)
        else:
            n = ref.shape[0]
            flat = staged.at[pl.ds(at, n * rows)]
            flat[...] = ref[...].reshape(n * rows, W)
            store(flat, at)

    store_blocks(early.o, 0)
    middle.stage4()
    late.stage4()
    middle.finish()
    store_blocks(middle.o, 1536)
    late.finish()
    store_blocks(late.o, 2560)
    for c in stores:
        c.wait()
    for x in links.all:
        x.wait_send()


def place(
    fine_h, node_h, edge_h, grads_h, fine_o, node_o, edge_o, fw_o, cw_o,
    fine, node, edge, grads, fwg, cwg, lsem, ssem,
):
    half = edge.shape[0] // 2
    parts = [(grads_h, grads, None), (fine_h, fine, fine_o), (node_h, node, node_o)]
    for i in range(2):
        rows = pl.ds(half * i, half)
        parts.append((edge_h.at[rows], edge.at[rows], edge_o.at[rows]))
    loads = [pltpu.make_async_copy(a, b, lsem.at[i]) for i, (a, b, c) in enumerate(parts)]
    moves = [pltpu.make_async_copy(b, c, ssem.at[i]) for i, (a, b, c) in enumerate(parts) if i > 0]
    for c in loads:
        c.start()
    for c, m in zip(loads[1:], moves):
        c.wait()
        m.start()
    loads[0].wait()

    def scaled(at, rows, scale):
        return grads[at:at + rows].astype(F32) * scale

    cwg[0:256] = scaled(0, 256, COARSE_SCALE)
    cwg[256:768] = scaled(1280, 512, COARSE_SCALE)
    cwg[768:1792] = scaled(256, 1024, COARSE_SCALE)
    fwg[0:256] = scaled(2560, 256, FINE_SCALE)
    fwg[256:768] = scaled(3072, 512, FINE_SCALE)
    fwg[768:1024] = scaled(2816, 256, FINE_SCALE)
    fwg[1024:1792] = scaled(1792, 768, FINE_SCALE)
    last = [pltpu.make_async_copy(fwg, fw_o, ssem.at[5]), pltpu.make_async_copy(cwg, cw_o, ssem.at[6])]
    for c in last:
        c.start()
    for c in moves + last:
        c.wait()


def body(
    nodes, edges, senders, receivers, edge_count, halo_rows, aggregates,
    coarse_edges, coarse_senders, coarse_receivers, cotangent, fine_weights, coarse_weights,
):
    vm = pl.BlockSpec(memory_space=pltpu.VMEM)
    hbm = pl.BlockSpec(memory_space=pl.ANY)
    V = pltpu.VMEM
    scratch = [
        V((1024, W), BF),
        V((4096, W), BF),
        V((1024, W), BF),
        V((1792, W), BF),
        V((1792, W), BF),
        V((512, W), BF),
        V((16, 128), jnp.int32),
        V((8, 128), jnp.int32),
        V((512, 1024), BF),
        V((16, 32, W), BF),
        V((16, 32, W), BF),
        V((2, 512, 1024), BF),
        V((8, 13, 512, 128), BF),
        V((8, 512, 128), BF),
        V((1792, W), BF),
        V((1024, W), BF),
        V((4096, W), BF),
        V((4096, W), BF),
        V((4096, W), BF),
        V((4096, 1), F32),
        V((1024, W), BF),
        V((1024, W), BF),
        V((1024, W), BF),
        V((1024, W), BF),
        V((1024, 1), F32),
        V((1024, W), BF),
        V((8, 128, W), BF),
        V((512, 128), BF),
        V((1408, W), BF),
        V((512, W), BF),
        V((512, W), BF),
        V((512, W), BF),
        V((512, 1), F32),
        V((8, 128, W), BF),
        V((8, 128, W), BF),
        V((1024, W), BF),
        V((4096, W), F32),
        V((1024, W), BF),
        V((1024, W), BF),
        V((16, 32, W), BF),
        V((16, 32, W), BF),
        pltpu.SemaphoreType.DMA((256,)),
        pltpu.SemaphoreType.DMA((256,)),
        pltpu.SemaphoreType.DMA((6,)),
        pltpu.SemaphoreType.DMA((12,)),
    ]
    for _ in range(3):
        scratch += [V((2, YS, 128, W), BF), V((YS, 128, W), BF), V((YS, 128, W), BF), V((YS, 128, W), BF)]
    for rows in (48, 32, 32):
        scratch += [V((2, DOM, rows, W), BF), V((DOM, rows, W), BF), V((DOM, rows, W), BF),
                    V((DOM, rows, W), BF), V((YS, rows, W), BF), V((2, DOM, rows, W), BF)]
    shape = jax.ShapeDtypeStruct
    fine_out, node_grad, edge_grad, grads = pl.pallas_call(
        kernel,
        out_shape=(shape((1024, W), BF), shape((1024, W), BF), shape((4096, W), BF), shape((3584, W), BF)),
        in_specs=[hbm, hbm, vm, vm, pl.BlockSpec(memory_space=pltpu.SMEM), vm, vm,
                  hbm, vm, vm, hbm, hbm, hbm],
        out_specs=(hbm,) * 4,
        scratch_shapes=scratch,
        compiler_params=pltpu.CompilerParams(
            collective_id=0, has_side_effects=True, vmem_limit_bytes=64 * 1024 * 1024 - 65536
        ),
    )(
        nodes, edges, senders.reshape(32, 128), receivers.reshape(32, 128), edge_count,
        halo_rows.reshape(16, 32), aggregates.reshape(8, 128), coarse_edges,
        coarse_senders.reshape(32, 128), coarse_receivers.reshape(32, 128), cotangent,
        fine_weights, coarse_weights,
    )
    return pl.pallas_call(
        place,
        out_shape=(shape((1024, W), BF), shape((1024, W), BF), shape((4096, W), BF),
                   shape((1792, W), F32), shape((1792, W), F32)),
        in_specs=[hbm] * 4,
        out_specs=(hbm,) * 5,
        scratch_shapes=[V((1024, W), BF), V((1024, W), BF), V((4096, W), BF), V((3584, W), BF), V((1792, W), F32),
                        V((1792, W), F32), pltpu.SemaphoreType.DMA((5,)), pltpu.SemaphoreType.DMA((7,))],
        compiler_params=pltpu.CompilerParams(vmem_limit_bytes=62 * 1024 * 1024),
    )(fine_out, node_grad, edge_grad, grads)


def solution(mesh):
    both = ("dom", "grp")
    placed = (
        P(both, None), P(both, None), P(both), P(both), P(both), P(both, None, None), P(both),
        P("dom", None, None), P("dom", None), P("dom", None), P(both, None), P(), P(),
    )
    return jax.shard_map(
        body, mesh=mesh, in_specs=placed,
        out_specs=(P(both, None), P(both, None), P(both, None), P(), P()),
        check_vma=False,
    )
```

```python
import jax
import jax.numpy as jnp
from jax import lax
from jax.experimental import pallas as pl
from jax.experimental.pallas import tpu as pltpu
from jax.sharding import PartitionSpec as P

MESH = pl.DeviceIdType.MESH
BF = jnp.bfloat16
F32 = jnp.float32
W = 256
DOM = 16
GRP = 8
TILES = 8
YS = 4
BIG = 2048
FINE_SCALE = 524288 ** (-0.5)
COARSE_SCALE = 65536 ** (-0.5)


def mm(a, b):
    return jnp.dot(a, b, preferred_element_type=F32)


def mm_nt(a, b):
    return lax.dot_general(a, b, (((1,), (1,)), ((), ())), preferred_element_type=F32)


def mm_tn(a, b):
    return lax.dot_general(a, b, (((0,), (0,)), ((), ())), preferred_element_type=F32)


def iota(shape, axis):
    return lax.broadcasted_iota(jnp.int32, shape, axis)


def hot(mask):
    return jnp.where(mask, 1.0, 0.0).astype(BF)


def hot16(mask):
    return jnp.where(mask, jnp.ones(mask.shape, BF), jnp.zeros(mask.shape, BF))


def column(row):
    return jnp.broadcast_to(row, (128, 128)).T


def silu_parts(h):
    sig = 1.0 / (1.0 + jnp.exp(-h))
    active = h * sig
    return active.astype(BF), (sig * (1.0 + h - active)).astype(BF)


def norm(z):
    centre = z - jnp.mean(z, axis=-1, keepdims=True)
    rs = lax.rsqrt(jnp.mean(centre * centre, axis=-1, keepdims=True) + 1e-05)
    return centre * rs, rs


def norm_back(dy, y, rs):
    first = jnp.mean(dy, axis=-1, keepdims=True)
    second = jnp.mean(dy * y, axis=-1, keepdims=True)
    return (rs * (dy - first - y * second)).astype(BF)


def norm_back_centred(dy, y, rs):
    second = jnp.mean(dy * y, axis=-1, keepdims=True)
    return (rs * (dy - y * second)).astype(BF)


def turn(ref, rows, count):
    def step(i, c):
        block = pl.ds(pl.multiple_of(rows + 256 * i, 256), 256)
        ref[block, :] = ref[block, :].T
        return c

    lax.fori_loop(0, count, step, 0)


def mm_turned(ref, rows, count, b):
    left = [ref[rows + 256 * i:rows + 256 * i + 256, :] for i in range(count)]
    return mm(jnp.concatenate(left, axis=1), b)


class Links:
    def __init__(self, ssem, rsem):
        self.d, self.g = lax.axis_index("dom"), lax.axis_index("grp")
        self.y, self.core = self.g // 2, lax.rem(self.g, 2)
        self.ssem, self.rsem, self.used = ssem, rsem, 0
        self.all = []

    def exchange(self, kind, src, dst):
        x = Exchange(self, kind, src, dst, self.used)
        self.used += x.count
        self.all.append(x)
        return x


class Exchange:
    def __init__(self, at, kind, src, dst, off):
        self.at, self.kind, self.src, self.dst, self.off = at, kind, src, dst, off
        self.count = {"dom": DOM, "grp": GRP, "y": YS, "mate": 2}[kind]

    def copy(self, k):
        at = self.at
        if self.kind == "dom":
            p = lax.rem(at.d + k, DOM)
            device = {"dom": p}
        elif self.kind == "grp":
            p = lax.rem(at.g + k, GRP)
            device = {"grp": p}
        elif self.kind == "y":
            p = lax.rem(at.y + k, YS)
            device = {"grp": 2 * p + at.core}
        else:
            p = 1 - at.core
            device = {"grp": 2 * at.y + p}
        return pltpu.make_async_remote_copy(
            src_ref=self.src(p),
            dst_ref=self.dst(k),
            send_sem=self.at.ssem.at[self.off + k],
            recv_sem=self.at.rsem.at[self.off + k],
            device_id=device,
            device_id_type=MESH,
        )

    def each(self, act):
        def step(k, carry):
            act(self.copy(k))
            return carry

        for k in sorted(range(1, self.count), key=lambda k: abs(k - self.count // 2)):
            step(k, 0)

    def start(self):
        self.each(lambda c: c.start())

    def wait_recv(self):
        self.each(lambda c: c.wait_recv())

    def wait_send(self):
        self.each(lambda c: c.wait_send())


def total_of(first, blocks, which):
    total = first.astype(F32)
    for k in which:
        total = total + blocks[k].astype(F32)
    return total


class GroupSum:
    def __init__(self, links, s, m, t, r):
        self.links, self.s, self.m, self.t, self.r = links, s, m, t, r
        self.first = links.exchange("mate", lambda p: s.at[p], lambda k: m)
        self.second = links.exchange("y", lambda p: t.at[p], lambda k: r.at[k])

    def pair(self):
        self.first.wait_recv()
        self.t[...] = (self.s[self.links.core].astype(F32) + self.m[...].astype(F32)).astype(BF)
        self.second.start()

    def result(self):
        self.second.wait_recv()
        return total_of(self.t[self.links.y], self.r, range(1, YS))


class GroupGather:
    def __init__(self, links, b):
        self.links, self.b = links, b
        g, y, core = links.g, links.y, links.core
        self.mate = links.exchange("mate", lambda p: b.at[g], lambda k: b.at[g])
        self.far = links.exchange("y", lambda p: b.at[g], lambda k: b.at[g])
        self.passed = []
        for k in range(1, YS):
            p = 2 * lax.rem(y + YS - k, YS) + core
            self.passed.append(links.exchange("mate", lambda q, p=p: b.at[p], lambda q, p=p: b.at[p]))

    def start(self):
        self.far.start()
        self.mate.start()

    def wait_recv(self):
        for k in range(1, YS):
            self.far.copy(k).wait_recv()
            self.passed[k - 1].start()
        self.mate.wait_recv()
        for x in self.passed:
            x.wait_recv()


class AllSum:
    def __init__(self, links, s, m, t, r, v, o):
        self.links, self.s, self.m, self.t, self.r, self.v, self.o = links, s, m, t, r, v, o
        d, y, core = links.d, links.y, links.core
        self.x0 = links.exchange("mate", lambda p: s.at[p], lambda k: m)
        self.x1 = links.exchange("dom", lambda p: t.at[p], lambda k: r.at[k])
        self.x2 = links.exchange("y", lambda p: v.at[y], lambda k: v.at[y])
        self.x3 = links.exchange("dom", lambda p: o.at[core, d], lambda k: o.at[core, d])
        self.x4 = links.exchange("mate", lambda p: o.at[core], lambda k: o.at[core])

    def stage0(self):
        self.x0.start()

    def stage1(self):
        self.x0.wait_recv()
        self.t[...] = (self.s[self.links.core].astype(F32) + self.m[...].astype(F32)).astype(BF)
        self.x1.start()

    def stage2(self):
        self.x1.wait_recv()
        self.v[self.links.y] = total_of(self.t[self.links.d], self.r, range(1, DOM)).astype(BF)
        self.x2.start()

    def stage3(self):
        self.x2.wait_recv()
        self.o[self.links.core, self.links.d] = total_of(self.v[0], self.v, range(1, YS)).astype(BF)
        self.x3.start()

    def stage4(self):
        self.x3.wait_recv()
        self.x4.start()

    def finish(self):
        self.x4.wait_recv()


def put(ref, lead, at, value):
    value = value.astype(BF)
    rows, pos = ref.shape[-2], 0
    while pos < value.shape[0]:
        block, inside = (at + pos) // rows, (at + pos) % rows
        n = min(rows - inside, value.shape[0] - pos)
        ref[lead(block) + (slice(inside, inside + n), slice(None))] = value[pos:pos + n]
        pos += n


def halves(block):
    return (block // DOM, block % DOM)


def kernel(
    nodes_h, edges_h, snd, rcv, cnt, halo, agg, cedges_h, csnd, crcv, cot_h, fw_h, cw_h,
    fine_out_h, node_grad_h, edge_grad_h, grads_h, *s
):
    (nodes, edges, cot, fw, cw, ce,
     hpad, hr, ohh, outg, hin, m_t, oh, ohr, wcat, p_r, act, gpr, yv, rsv, summed,
     an, gn, yn, rsn, refined, cinb, cx, cwc, cact, cgp, cy, crs, coutb,
     dcinb, rg, work, dsm, s_r, hret, hrin, ssem, rsem, isem, osem) = s[:45]
    rest = list(s[45:])
    edge_grad, staged, fine_out, node_grad = yv, act, refined, rg
    s_s, dnp = work.at[0:1536], work.at[1536:2560]
    g_ae, g_b = work.at[2560:2816], work.at[2816:3072]

    def take(n):
        out = rest[:n]
        del rest[:n]
        return out

    links = Links(ssem, rsem)
    d, g, y, core = links.d, links.g, links.y, links.core
    count = cnt[0]

    loads = [
        pltpu.make_async_copy(src, dst, isem.at[i])
        for i, (src, dst) in enumerate((
            (nodes_h, nodes), (fw_h, fw), (cot_h, cot), (edges_h, edges), (cw_h, cw),
            (cedges_h.at[0, pl.ds(pl.multiple_of(g * 512, 512), 512)], ce),
        ))
    ]
    for c in loads:
        c.start()
    ld_nodes, ld_fw, ld_cot, ld_edges, ld_cw, ld_ce = loads
    barrier = pltpu.get_barrier_semaphore()

    def greet_dom(k, c):
        pl.semaphore_signal(barrier, inc=1, device_id={"dom": lax.rem(d + k, DOM)}, device_id_type=MESH)
        return c

    def greet_grp(k, c):
        pl.semaphore_signal(barrier, inc=1, device_id={"grp": lax.rem(g + k, GRP)}, device_id_type=MESH)
        return c

    lax.fori_loop(1, DOM, greet_dom, 0)
    lax.fori_loop(1, GRP, greet_grp, 0)

    x_halo = links.exchange("dom", lambda p: outg.at[p], lambda k: hin.at[d])
    x_ret = links.exchange("dom", lambda p: hret.at[p], lambda k: hrin.at[d])
    pro = GroupSum(links, *take(4))
    res = GroupSum(links, *take(4))
    sen = GroupSum(links, *take(4))
    x_cin = GroupGather(links, cinb)
    x_cout = GroupGather(links, coutb)
    x_dcin = GroupGather(links, dcinb)
    early = AllSum(links, *take(6))
    middle = AllSum(links, *take(6))
    late = AllSum(links, *take(6))

    lane = iota((128, 128), 1)
    sub = iota((128, 128), 0)
    lane16 = lane.astype(jnp.int16)
    sub16 = sub.astype(jnp.int16)

    hpad[...] = jnp.zeros_like(hpad)
    hpad[:, 0:32] = halo[...]
    padded = hpad[...]
    rolled = [padded] + [pltpu.roll(padded, 32 * i, 1) for i in range(1, 4)]
    for j in range(4):
        row = rolled[0][4 * j:4 * j + 1]
        for i in range(1, 4):
            row = row + rolled[i][4 * j + i:4 * j + i + 1]
        hr[j:j + 1, :] = row
        col = column(row)
        for b in range(8):
            ohh[128 * j:128 * j + 128, 128 * b:128 * b + 128] = hot(col == lane + 128 * b)
    hin[d] = jnp.zeros((32, W), BF)
    hrin[d] = jnp.zeros((32, W), BF)
    ld_nodes.wait()
    outg[...] = mm(ohh[...], nodes[...]).astype(BF).reshape(16, 32, W)
    pl.semaphore_wait(barrier, DOM + GRP - 2)
    x_halo.start()

    def member(j, c):
        row = agg[pl.ds(j, 1), :]
        at = pl.multiple_of(j * 128, 128)
        for b in range(8):
            m_t[b % 2, 128 * (b // 2):128 * (b // 2) + 128, pl.ds(at, 128)] = hot(sub + 128 * b == row)
        return c

    lax.fori_loop(0, 8, member, 0)
    ld_cot.wait()
    for h in range(2):
        pro.s[h] = mm(m_t[h], cot[...]).astype(BF).reshape(YS, 128, W)
    pro.first.start()

    ld_fw.wait()
    wcat[0:256] = fw[0:256]
    wcat[256:1280] = mm(nodes[...], fw[256:512]).astype(BF)
    p_r[...] = mm(nodes[...], fw[512:768]).astype(BF)

    def edge_hot(t, c):
        for j in range(4):
            rows = slice(128 * j, 128 * j + 128)
            scol = column(snd[pl.ds(4 * t + j, 1), :]).astype(jnp.int16)
            rcol = column(rcv[pl.ds(4 * t + j, 1), :] - 128 * t)
            for b in range(12):
                oh[t, b, rows, :] = hot16(scol == lane16 + jnp.int16(128 * b))
            ohr[t, rows, :] = hot((rcol == lane) & (sub + 128 * j < count))
        return c

    lax.fori_loop(0, TILES, edge_hot, 0, unroll=2)
    pro.pair()
    ld_edges.wait()

    def edge_local(i, c):
        rows = pl.ds(pl.multiple_of(i * BIG, BIG), BIG)
        tiles = [i * (BIG // 512) + q for q in range(BIG // 512)]
        far = [jnp.concatenate([oh[t, b] for b in range(8)], axis=1) for t in tiles]
        near = [mm(ohr[t], p_r[pl.ds(pl.multiple_of(t * 128, 128), 128), :]) for t in tiles]
        joined = jnp.concatenate([edges[rows, :], jnp.concatenate(far, axis=0)], axis=1)
        work[rows, :] = mm(joined, wcat[0:1280]) + jnp.concatenate(near, axis=0)
        return c

    lax.fori_loop(0, 4096 // BIG, edge_local, 0)
    x_halo.wait_recv()
    wcat[1280:1792] = mm(hin[...].reshape(512, W), fw[256:512]).astype(BF)

    def edge_forward(i, c):
        rows = pl.ds(pl.multiple_of(i * BIG, BIG), BIG)
        tiles = [i * (BIG // 512) + q for q in range(BIG // 512)]
        far = [jnp.concatenate([oh[t, b] for b in range(8, 12)], axis=1) for t in tiles]
        a, gp = silu_parts(work[rows, :] + mm(jnp.concatenate(far, axis=0), wcat[1280:1792]))
        act[rows, :] = a
        gpr[rows, :] = gp
        y, rs = norm(mm(a, fw[768:1024]))
        yv[rows, :] = y.astype(BF)
        rsv[rows, :] = rs
        return c

    def edge_sum(t, c):
        back = []
        for j in range(4):
            rrow = rcv[pl.ds(4 * t + j, 1), :] - 128 * t
            back.append(hot((rrow == sub) & (lane + 128 * j < count)))
        rows = pl.ds(pl.multiple_of(t * 512, 512), 512)
        summed[pl.ds(pl.multiple_of(t * 128, 128), 128), :] = mm(
            jnp.concatenate(back, axis=1), yv[rows, :]).astype(BF)
        return c

    lax.fori_loop(0, 4096 // BIG, edge_forward, 0)
    lax.fori_loop(0, TILES, edge_sum, 0, unroll=TILES)

    a, gp = silu_parts(mm(nodes[...], fw[1024:1280]) + mm(summed[...], fw[1280:1536]))
    an[...] = a
    gn[...] = gp
    ynode, rs = norm(mm(a, fw[1536:1792]))
    yn[...] = ynode.astype(BF)
    rsn[...] = rs
    refined[...] = (nodes[...].astype(F32) + ynode).astype(BF)
    hin_t = p_r
    hin_t[0:512] = hin[...].reshape(512, W)

    res.s[1 - core] = (mm(m_t[1 - core], refined[...]) * 0.125).astype(BF).reshape(YS, 128, W)
    res.first.start()
    res.s[core] = (mm(m_t[core], refined[...]) * 0.125).astype(BF).reshape(YS, 128, W)
    res.pair()

    def edge_hot_back(t, c):
        for j in range(4):
            rows = slice(128 * j, 128 * j + 128)
            srow = jnp.broadcast_to(snd[pl.ds(4 * t + j, 1), :], (128, 128)).astype(jnp.int16)
            rrow = rcv[pl.ds(4 * t + j, 1), :] - 128 * t
            for b in range(12):
                oh[t, b, rows, :] = hot16(srow == sub16 + jnp.int16(128 * b))
            oh[t, 12, rows, :] = hot((rrow == sub) & (lane + 128 * j < count))
        return c

    def member_back(j, c):
        col = column(agg[pl.ds(j, 1), :])
        for b in range(8):
            m_t[j // 4, pl.ds(pl.multiple_of(lax.rem(j, 4) * 128, 128), 128), 128 * b:128 * b + 128] = hot(col == lane + 128 * b)
        return c

    ld_ce.wait()
    ld_cw.wait()
    cback = []
    for j in range(4):
        srow = csnd[pl.ds(4 * g + j, 1), :]
        rrow = crcv[pl.ds(4 * g + j, 1), :]
        scol = column(srow)
        rcol = column(rrow)
        for b in range(8):
            m_t[0, 128 * j:128 * j + 128, 128 * b:128 * b + 128] = hot(scol == lane + 128 * b)
        cx[128 * j:128 * j + 128, :] = hot(rcol == lane)
        cback.append(hot(rrow == sub))
    cback = jnp.concatenate(cback, axis=1)
    cwc[0:256] = cw[0:256]
    pg = pro.result().astype(BF).astype(F32)
    lax.fori_loop(0, 3, edge_hot_back, 0)
    turn(nodes, 0, 4)
    turn(summed, 0, 4)
    turn(an, 0, 4)
    turn(hin_t, 0, 2)
    cin = res.result().astype(BF)
    cinb[g] = cin
    x_cin.start()
    cwc[1280:1408] = mm(cin, cw[512:768]).astype(BF)
    lax.fori_loop(3, TILES, edge_hot_back, 0)
    x_cin.wait_recv()
    cwc[256:1280] = mm(cinb[...].reshape(1024, W), cw[256:512]).astype(BF)
    ca, cg = silu_parts(mm(jnp.concatenate([ce[...], m_t[0], cx[...]], axis=1), cwc[...]))
    cact[...] = ca
    cgp[...] = cg
    cyn, rs = norm(mm(ca, cw[768:1024]))
    cyn = cyn.astype(BF)
    cy[...] = cyn
    crs[...] = rs
    csum = mm(cback, cyn).astype(BF)
    cna, cng = silu_parts(mm(cin, cw[1024:1280]) + mm(csum, cw[1280:1536]))
    cny, cnrs = norm(mm(cna, cw[1536:1792]))
    coutb[g] = (cin.astype(F32) + cny).astype(BF)

    cndz = norm_back(pg, cny, cnrs)
    cndh = (mm_nt(cndz, cw[1536:1792]) * cng.astype(F32)).astype(BF)
    dcin_part = pg + mm_nt(cndh, cw[1024:1280])
    dcsum = mm_nt(cndh, cw[1280:1536]).astype(BF)
    cdz = norm_back(mm(cx[...], dcsum), cy[...].astype(F32), crs[...])
    cdh = (mm_nt(cdz, cw[768:1024]) * cgp[...].astype(F32)).astype(BF)

    def sender_sum(half):
        blocks = []
        for p in range(YS):
            at = 128 * (2 * p + half)
            blocks.append(jnp.concatenate(
                [hot(csnd[pl.ds(4 * g + j, 1), :] - at == sub) for j in range(4)], axis=1))
        sen.s[half] = mm(jnp.concatenate(blocks, axis=0), cdh).astype(BF).reshape(YS, 128, W)

    sender_sum(1 - core)
    sen.first.start()
    sender_sum(core)
    s_cr = mm(cback, cdh).astype(BF)
    sen.pair()
    put(early.s, halves, 0, mm_tn(ce[...], cdh))
    put(early.s, halves, 256, mm_tn(cact[...], cdz))
    put(early.s, halves, 512, mm_tn(cin, cndh))
    put(early.s, halves, 768, mm_tn(csum, cndh))
    put(early.s, halves, 1024, mm_tn(cna, cndz))
    put(middle.s, halves, 0, mm_tn(cin, s_cr))
    dcin_part = dcin_part + mm_nt(s_cr, cw[512:768])
    lax.fori_loop(0, 8, member_back, 0)
    turn(edges, 0, 8)
    s_tot = sen.result().astype(BF)
    dcinb[g] = (dcin_part + mm_nt(s_tot, cw[256:512])).astype(BF)
    x_dcin.start()
    put(early.s, halves, 1280, mm_tn(cin, s_tot))
    early.stage0()

    early.stage1()
    turn(edges, 2048, 8)
    turn(act, 0, 16)
    x_dcin.wait_recv()
    x_cout.start()
    rg[...] = (cot[...].astype(F32) + 0.125 * mm(m_t[...].reshape(1024, 1024), dcinb[...].reshape(1024, W))).astype(BF)

    dz = norm_back(rg[...].astype(F32), yn[...].astype(F32), rsn[...])
    dh = (mm_nt(dz, fw[1536:1792]) * gn[...].astype(F32)).astype(BF)
    dnp[...] = rg[...].astype(F32) + mm_nt(dh, fw[1024:1280])
    dsum = mm_nt(dh, fw[1280:1536]).astype(BF).astype(F32)
    dsm[...] = (dsum - jnp.mean(dsum, axis=-1, keepdims=True)).astype(BF)
    put(middle.s, halves, 256, mm_turned(nodes, 0, 4, dh))
    put(middle.s, halves, 512, mm_turned(summed, 0, 4, dh))
    put(middle.s, halves, 768, mm_turned(an, 0, 4, dz))
    middle.stage0()
    early.stage2()

    s_s[...] = jnp.zeros_like(s_s)
    g_ae[...] = jnp.zeros_like(g_ae)
    g_b[...] = jnp.zeros_like(g_b)

    def edge_backward(i):
        base = i * BIG
        rows = pl.ds(base, BIG)
        tiles = [i * (BIG // 512) + q for q in range(BIG // 512)]
        dmsg = jnp.concatenate([mm(ohr[t], dsm[128 * t:128 * t + 128, :]) for t in tiles], axis=0)
        dz = norm_back_centred(dmsg, yv[rows, :].astype(F32), rsv[rows, :])
        dh = (mm_nt(dz, fw[768:1024]) * gpr[rows, :].astype(F32)).astype(BF)
        gpr[rows, :] = dh
        g_b[...] += mm_turned(act, base, BIG // 256, dz)
        g_ae[...] += mm_turned(edges, base, BIG // 256, dh)

        def turned(t, b):
            return jnp.concatenate([oh[t, b, 128 * j:128 * j + 128, :] for j in range(4)], axis=1)

        for q in range(3):
            part = [jnp.concatenate([turned(t, 4 * q + b) for t in tiles], axis=1) for b in range(4)]
            s_s[512 * q:512 * q + 512, :] += mm(jnp.concatenate(part, axis=0), dh)
        for q, t in enumerate(tiles):
            s_r[128 * t:128 * t + 128, :] = mm(turned(t, 12), dh[512 * q:512 * q + 512]).astype(BF)

    for i in range(4096 // BIG):
        if i == 4096 // BIG // 2:
            early.stage3()
            middle.stage1()
        edge_backward(i)

    put(late.s, halves, 0, g_ae[...])
    put(late.s, halves, 256, g_b[...])
    ss = s_s[...].astype(BF)
    put(late.s, halves, 512, mm_turned(nodes, 0, 4, ss[0:1024]) + mm_turned(hin_t, 0, 2, ss[1024:1536]))
    put(late.s, halves, 768, mm_turned(nodes, 0, 4, s_r[...]))
    late.stage0()
    hret[...] = mm_nt(ss[1024:1536], fw[256:512]).astype(BF).reshape(16, 32, W)
    late.stage1()
    x_ret.start()
    middle.stage2()
    early.stage4()

    for i in range(4096 // BIG):
        rows = pl.ds(i * BIG, BIG)
        edge_grad[rows, :] = mm_nt(gpr[rows, :], fw[0:256]).astype(BF)
    st_edge = pltpu.make_async_copy(edge_grad, edge_grad_h, osem.at[1])
    st_edge.start()
    x_cout.wait_recv()
    fine_out[...] = (refined[...].astype(F32) + mm(m_t[...].reshape(1024, 1024), coutb[...].reshape(1024, W))).astype(BF)
    st_fine = pltpu.make_async_copy(fine_out, fine_out_h, osem.at[0])
    st_fine.start()
    own = dnp[...] + mm_nt(ss[0:1024], fw[256:512]) + mm_nt(s_r[...], fw[512:768])
    late.stage2()
    middle.stage3()
    x_ret.wait_recv()
    node_grad[...] = (own + mm_tn(ohh[...], hrin[...].reshape(512, W))).astype(BF)
    st_node = pltpu.make_async_copy(node_grad, node_grad_h, osem.at[2])
    st_node.start()
    late.stage3()
    early.finish()
    stores = [st_fine, st_edge, st_node]

    def store(ref, at):
        rows = ref.shape[0]
        copy = pltpu.make_async_copy(ref, grads_h.at[pl.ds(at, rows)], osem.at[len(stores)])
        copy.start()
        stores.append(copy)

    def store_blocks(ref, at):
        rows = ref.shape[-2]
        if len(ref.shape) == 4:
            for h in range(2):
                store_blocks(ref.at[h], at + h * DOM * rows)
        else:
            n = ref.shape[0]
            flat = staged.at[pl.ds(at, n * rows)]
            flat[...] = ref[...].reshape(n * rows, W)
            store(flat, at)

    store_blocks(early.o, 0)
    middle.stage4()
    late.stage4()
    middle.finish()
    store_blocks(middle.o, 1536)
    late.finish()
    store_blocks(late.o, 2560)
    for c in stores:
        c.wait()
    for x in links.all:
        x.wait_send()


def place(
    fine_h, node_h, edge_h, grads_h, fine_o, node_o, edge_o, fw_o, cw_o,
    fine, node, edge, grads, fwg, cwg, lsem, ssem,
):
    half = edge.shape[0] // 2
    parts = [(grads_h, grads, None), (fine_h, fine, fine_o), (node_h, node, node_o)]
    for i in range(2):
        rows = pl.ds(half * i, half)
        parts.append((edge_h.at[rows], edge.at[rows], edge_o.at[rows]))
    loads = [pltpu.make_async_copy(a, b, lsem.at[i]) for i, (a, b, c) in enumerate(parts)]
    moves = [pltpu.make_async_copy(b, c, ssem.at[i]) for i, (a, b, c) in enumerate(parts) if i > 0]
    for c in loads:
        c.start()
    for c, m in zip(loads[1:], moves):
        c.wait()
        m.start()
    loads[0].wait()

    def scaled(at, rows, scale):
        return grads[at:at + rows].astype(F32) * scale

    cwg[0:256] = scaled(0, 256, COARSE_SCALE)
    cwg[256:768] = scaled(1280, 512, COARSE_SCALE)
    cwg[768:1792] = scaled(256, 1024, COARSE_SCALE)
    fwg[0:256] = scaled(2560, 256, FINE_SCALE)
    fwg[256:768] = scaled(3072, 512, FINE_SCALE)
    fwg[768:1024] = scaled(2816, 256, FINE_SCALE)
    fwg[1024:1792] = scaled(1792, 768, FINE_SCALE)
    last = [pltpu.make_async_copy(fwg, fw_o, ssem.at[5]), pltpu.make_async_copy(cwg, cw_o, ssem.at[6])]
    for c in last:
        c.start()
    for c in moves + last:
        c.wait()


def body(
    nodes, edges, senders, receivers, edge_count, halo_rows, aggregates,
    coarse_edges, coarse_senders, coarse_receivers, cotangent, fine_weights, coarse_weights,
):
    vm = pl.BlockSpec(memory_space=pltpu.VMEM)
    hbm = pl.BlockSpec(memory_space=pl.ANY)
    V = pltpu.VMEM
    scratch = [
        V((1024, W), BF),
        V((4096, W), BF),
        V((1024, W), BF),
        V((1792, W), BF),
        V((1792, W), BF),
        V((512, W), BF),
        V((16, 128), jnp.int32),
        V((8, 128), jnp.int32),
        V((512, 1024), BF),
        V((16, 32, W), BF),
        V((16, 32, W), BF),
        V((2, 512, 1024), BF),
        V((8, 13, 512, 128), BF),
        V((8, 512, 128), BF),
        V((1792, W), BF),
        V((1024, W), BF),
        V((4096, W), BF),
        V((4096, W), BF),
        V((4096, W), BF),
        V((4096, 1), F32),
        V((1024, W), BF),
        V((1024, W), BF),
        V((1024, W), BF),
        V((1024, W), BF),
        V((1024, 1), F32),
        V((1024, W), BF),
        V((8, 128, W), BF),
        V((512, 128), BF),
        V((1408, W), BF),
        V((512, W), BF),
        V((512, W), BF),
        V((512, W), BF),
        V((512, 1), F32),
        V((8, 128, W), BF),
        V((8, 128, W), BF),
        V((1024, W), BF),
        V((4096, W), F32),
        V((1024, W), BF),
        V((1024, W), BF),
        V((16, 32, W), BF),
        V((16, 32, W), BF),
        pltpu.SemaphoreType.DMA((256,)),
        pltpu.SemaphoreType.DMA((256,)),
        pltpu.SemaphoreType.DMA((6,)),
        pltpu.SemaphoreType.DMA((12,)),
    ]
    for _ in range(3):
        scratch += [V((2, YS, 128, W), BF), V((YS, 128, W), BF), V((YS, 128, W), BF), V((YS, 128, W), BF)]
    for rows in (48, 32, 32):
        scratch += [V((2, DOM, rows, W), BF), V((DOM, rows, W), BF), V((DOM, rows, W), BF),
                    V((DOM, rows, W), BF), V((YS, rows, W), BF), V((2, DOM, rows, W), BF)]
    shape = jax.ShapeDtypeStruct
    fine_out, node_grad, edge_grad, grads = pl.pallas_call(
        kernel,
        out_shape=(shape((1024, W), BF), shape((1024, W), BF), shape((4096, W), BF), shape((3584, W), BF)),
        in_specs=[hbm, hbm, vm, vm, pl.BlockSpec(memory_space=pltpu.SMEM), vm, vm,
                  hbm, vm, vm, hbm, hbm, hbm],
        out_specs=(hbm,) * 4,
        scratch_shapes=scratch,
        compiler_params=pltpu.CompilerParams(
            collective_id=0, has_side_effects=True, vmem_limit_bytes=64 * 1024 * 1024 - 65536
        ),
    )(
        nodes, edges, senders.reshape(32, 128), receivers.reshape(32, 128), edge_count,
        halo_rows.reshape(16, 32), aggregates.reshape(8, 128), coarse_edges,
        coarse_senders.reshape(32, 128), coarse_receivers.reshape(32, 128), cotangent,
        fine_weights, coarse_weights,
    )
    return pl.pallas_call(
        place,
        out_shape=(shape((1024, W), BF), shape((1024, W), BF), shape((4096, W), BF),
                   shape((1792, W), F32), shape((1792, W), F32)),
        in_specs=[hbm] * 4,
        out_specs=(hbm,) * 5,
        scratch_shapes=[V((1024, W), BF), V((1024, W), BF), V((4096, W), BF), V((3584, W), BF), V((1792, W), F32),
                        V((1792, W), F32), pltpu.SemaphoreType.DMA((5,)), pltpu.SemaphoreType.DMA((7,))],
        compiler_params=pltpu.CompilerParams(vmem_limit_bytes=62 * 1024 * 1024),
    )(fine_out, node_grad, edge_grad, grads)


def solution(mesh):
    both = ("dom", "grp")
    placed = (
        P(both, None), P(both, None), P(both), P(both), P(both), P(both, None, None), P(both),
        P("dom", None, None), P("dom", None), P("dom", None), P(both, None), P(), P(),
    )
    return jax.shard_map(
        body, mesh=mesh, in_specs=placed,
        out_specs=(P(both, None), P(both, None), P(both, None), P(), P()),
        check_vma=False,
    )
```

```python
import jax
import jax.numpy as jnp
from jax import lax
from jax.experimental import pallas as pl
from jax.experimental.pallas import tpu as pltpu
from jax.sharding import PartitionSpec as P

MESH = pl.DeviceIdType.MESH
BF = jnp.bfloat16
F32 = jnp.float32
W = 256
DOM = 16
GRP = 8
TILES = 8
YS = 4
BIG = 2048
FINE_SCALE = 524288 ** (-0.5)
COARSE_SCALE = 65536 ** (-0.5)


def mm(a, b):
    return jnp.dot(a, b, preferred_element_type=F32)


def mm_nt(a, b):
    return lax.dot_general(a, b, (((1,), (1,)), ((), ())), preferred_element_type=F32)


def mm_tn(a, b):
    return lax.dot_general(a, b, (((0,), (0,)), ((), ())), preferred_element_type=F32)


def iota(shape, axis):
    return lax.broadcasted_iota(jnp.int32, shape, axis)


def hot(mask):
    return jnp.where(mask, 1.0, 0.0).astype(BF)


def hot16(mask):
    return jnp.where(mask, jnp.ones(mask.shape, BF), jnp.zeros(mask.shape, BF))


def column(row):
    return jnp.broadcast_to(row, (128, 128)).T


def silu_parts(h):
    sig = 1.0 / (1.0 + jnp.exp(-h))
    active = h * sig
    return active.astype(BF), (sig * (1.0 + h - active)).astype(BF)


def norm(z):
    centre = z - jnp.mean(z, axis=-1, keepdims=True)
    rs = lax.rsqrt(jnp.mean(centre * centre, axis=-1, keepdims=True) + 1e-05)
    return centre * rs, rs


def norm_back(dy, y, rs):
    first = jnp.mean(dy, axis=-1, keepdims=True)
    second = jnp.mean(dy * y, axis=-1, keepdims=True)
    return (rs * (dy - first - y * second)).astype(BF)


def norm_back_centred(dy, y, rs):
    second = jnp.mean(dy * y, axis=-1, keepdims=True)
    return (rs * (dy - y * second)).astype(BF)


def turn(ref, rows, count):
    def step(i, c):
        block = pl.ds(pl.multiple_of(rows + 256 * i, 256), 256)
        ref[block, :] = ref[block, :].T
        return c

    lax.fori_loop(0, count, step, 0)


def mm_turned(ref, rows, count, b):
    left = [ref[rows + 256 * i:rows + 256 * i + 256, :] for i in range(count)]
    return mm(jnp.concatenate(left, axis=1), b)


class Links:
    def __init__(self, ssem, rsem):
        self.d, self.g = lax.axis_index("dom"), lax.axis_index("grp")
        self.y, self.core = self.g // 2, lax.rem(self.g, 2)
        self.ssem, self.rsem, self.used = ssem, rsem, 0
        self.all = []

    def exchange(self, kind, src, dst):
        x = Exchange(self, kind, src, dst, self.used)
        self.used += x.count
        self.all.append(x)
        return x


class Exchange:
    def __init__(self, at, kind, src, dst, off):
        self.at, self.kind, self.src, self.dst, self.off = at, kind, src, dst, off
        self.count = {"dom": DOM, "grp": GRP, "y": YS, "mate": 2}[kind]

    def copy(self, k):
        at = self.at
        if self.kind == "dom":
            p = lax.rem(at.d + k, DOM)
            device = {"dom": p}
        elif self.kind == "grp":
            p = lax.rem(at.g + k, GRP)
            device = {"grp": p}
        elif self.kind == "y":
            p = lax.rem(at.y + k, YS)
            device = {"grp": 2 * p + at.core}
        else:
            p = 1 - at.core
            device = {"grp": 2 * at.y + p}
        return pltpu.make_async_remote_copy(
            src_ref=self.src(p),
            dst_ref=self.dst(k),
            send_sem=self.at.ssem.at[self.off + k],
            recv_sem=self.at.rsem.at[self.off + k],
            device_id=device,
            device_id_type=MESH,
        )

    def each(self, act):
        def step(k, carry):
            act(self.copy(k))
            return carry

        for k in sorted(range(1, self.count), key=lambda k: abs(k - self.count // 2)):
            step(k, 0)

    def start(self):
        self.each(lambda c: c.start())

    def wait_recv(self):
        self.each(lambda c: c.wait_recv())

    def wait_send(self):
        self.each(lambda c: c.wait_send())


def total_of(first, blocks, which):
    total = first.astype(F32)
    for k in which:
        total = total + blocks[k].astype(F32)
    return total


class GroupSum:
    def __init__(self, links, s, m, t, r):
        self.links, self.s, self.m, self.t, self.r = links, s, m, t, r
        self.order = [2, 1, 3, 0]
        self.first = {}
        for k in self.order:
            q = lax.rem(links.y + k, YS)
            self.first[k] = links.exchange("mate", lambda p, q=q: s.at[p, q], lambda i, q=q: m.at[q])
        self.second = links.exchange("y", lambda p: t.at[p], lambda k: r.at[k])

    def start(self):
        for k in self.order:
            self.first[k].start()

    def pair(self):
        y, core = self.links.y, self.links.core
        for k in self.order:
            self.first[k].wait_recv()
            q = lax.rem(y + k, YS)
            self.t[q] = (self.s[core, q].astype(F32) + self.m[q].astype(F32)).astype(BF)
            if k > 0:
                self.second.copy(k).start()

    def result(self):
        self.second.wait_recv()
        return total_of(self.t[self.links.y], self.r, range(1, YS))


class GroupGather:
    def __init__(self, links, b):
        self.links, self.b = links, b
        g, y, core = links.g, links.y, links.core
        self.mate = links.exchange("mate", lambda p: b.at[g], lambda k: b.at[g])
        self.far = links.exchange("y", lambda p: b.at[g], lambda k: b.at[g])
        self.passed = []
        for k in range(1, YS):
            p = 2 * lax.rem(y + YS - k, YS) + core
            self.passed.append(links.exchange("mate", lambda q, p=p: b.at[p], lambda q, p=p: b.at[p]))

    def start(self):
        self.far.start()
        self.mate.start()

    def wait_recv(self):
        for k in range(1, YS):
            self.far.copy(k).wait_recv()
            self.passed[k - 1].start()
        self.mate.wait_recv()
        for x in self.passed:
            x.wait_recv()


class AllSum:
    def __init__(self, links, s, m, t, r, v, o):
        self.links, self.s, self.m, self.t, self.r, self.v, self.o = links, s, m, t, r, v, o
        d, y, core = links.d, links.y, links.core
        self.x0 = links.exchange("mate", lambda p: s.at[p], lambda k: m)
        self.x1 = links.exchange("dom", lambda p: t.at[p], lambda k: r.at[k])
        self.x2 = links.exchange("y", lambda p: v.at[y], lambda k: v.at[y])
        self.x3 = links.exchange("dom", lambda p: o.at[core, d], lambda k: o.at[core, d])
        self.x4 = links.exchange("mate", lambda p: o.at[core], lambda k: o.at[core])

    def stage0(self):
        self.x0.start()

    def stage1(self):
        self.x0.wait_recv()
        self.t[...] = (self.s[self.links.core].astype(F32) + self.m[...].astype(F32)).astype(BF)
        self.x1.start()

    def stage2(self):
        self.x1.wait_recv()
        self.v[self.links.y] = total_of(self.t[self.links.d], self.r, range(1, DOM)).astype(BF)
        self.x2.start()

    def stage3(self):
        self.x2.wait_recv()
        self.o[self.links.core, self.links.d] = total_of(self.v[0], self.v, range(1, YS)).astype(BF)
        self.x3.start()

    def stage4(self):
        self.x3.wait_recv()
        self.x4.start()

    def finish(self):
        self.x4.wait_recv()


def put(ref, lead, at, value):
    value = value.astype(BF)
    rows, pos = ref.shape[-2], 0
    while pos < value.shape[0]:
        block, inside = (at + pos) // rows, (at + pos) % rows
        n = min(rows - inside, value.shape[0] - pos)
        ref[lead(block) + (slice(inside, inside + n), slice(None))] = value[pos:pos + n]
        pos += n


def halves(block):
    return (block // DOM, block % DOM)


def kernel(
    nodes_h, edges_h, snd, rcv, cnt, halo, agg, cedges_h, csnd, crcv, cot_h, fw_h, cw_h,
    fine_out_h, node_grad_h, edge_grad_h, grads_h, *s
):
    (nodes, edges, cot, fw, cw, ce,
     hpad, hr, ohh, outg, hin, m_t, oh, ohr, wcat, p_r, act, gpr, yv, rsv, summed,
     an, gn, yn, rsn, refined, cinb, cx, cwc, cact, cgp, cy, crs, coutb,
     dcinb, rg, work, dsm, s_r, hret, hrin, ssem, rsem, isem, osem) = s[:45]
    rest = list(s[45:])
    edge_grad, staged, fine_out, node_grad = yv, act, refined, rg
    s_s, dnp = work.at[0:1536], work.at[1536:2560]
    g_ae, g_b = work.at[2560:2816], work.at[2816:3072]

    def take(n):
        out = rest[:n]
        del rest[:n]
        return out

    links = Links(ssem, rsem)
    d, g, y, core = links.d, links.g, links.y, links.core
    count = cnt[0]

    loads = [
        pltpu.make_async_copy(src, dst, isem.at[i])
        for i, (src, dst) in enumerate((
            (nodes_h, nodes), (fw_h, fw), (cot_h, cot), (edges_h, edges), (cw_h, cw),
            (cedges_h.at[0, pl.ds(pl.multiple_of(g * 512, 512), 512)], ce),
        ))
    ]
    for c in loads:
        c.start()
    ld_nodes, ld_fw, ld_cot, ld_edges, ld_cw, ld_ce = loads
    barrier = pltpu.get_barrier_semaphore()

    def greet_dom(k, c):
        pl.semaphore_signal(barrier, inc=1, device_id={"dom": lax.rem(d + k, DOM)}, device_id_type=MESH)
        return c

    def greet_grp(k, c):
        pl.semaphore_signal(barrier, inc=1, device_id={"grp": lax.rem(g + k, GRP)}, device_id_type=MESH)
        return c

    lax.fori_loop(1, DOM, greet_dom, 0)
    lax.fori_loop(1, GRP, greet_grp, 0)

    x_halo = links.exchange("dom", lambda p: outg.at[p], lambda k: hin.at[d])
    x_ret = links.exchange("dom", lambda p: hret.at[p], lambda k: hrin.at[d])
    pro = GroupSum(links, *take(4))
    res = GroupSum(links, *take(4))
    sen = GroupSum(links, *take(4))
    x_cin = GroupGather(links, cinb)
    x_cout = GroupGather(links, coutb)
    x_dcin = GroupGather(links, dcinb)
    early = AllSum(links, *take(6))
    middle = AllSum(links, *take(6))
    late = AllSum(links, *take(6))

    lane = iota((128, 128), 1)
    sub = iota((128, 128), 0)
    lane16 = lane.astype(jnp.int16)
    sub16 = sub.astype(jnp.int16)

    hpad[...] = jnp.zeros_like(hpad)
    hpad[:, 0:32] = halo[...]
    padded = hpad[...]
    rolled = [padded] + [pltpu.roll(padded, 32 * i, 1) for i in range(1, 4)]
    for j in range(4):
        row = rolled[0][4 * j:4 * j + 1]
        for i in range(1, 4):
            row = row + rolled[i][4 * j + i:4 * j + i + 1]
        hr[j:j + 1, :] = row
        col = column(row)
        for b in range(8):
            ohh[128 * j:128 * j + 128, 128 * b:128 * b + 128] = hot(col == lane + 128 * b)
    hin[d] = jnp.zeros((32, W), BF)
    hrin[d] = jnp.zeros((32, W), BF)
    ld_nodes.wait()
    outg[...] = mm(ohh[...], nodes[...]).astype(BF).reshape(16, 32, W)
    pl.semaphore_wait(barrier, DOM + GRP - 2)
    x_halo.start()

    def member(j, c):
        row = agg[pl.ds(j, 1), :]
        at = pl.multiple_of(j * 128, 128)
        for b in range(8):
            m_t[b % 2, 128 * (b // 2):128 * (b // 2) + 128, pl.ds(at, 128)] = hot(sub + 128 * b == row)
        return c

    lax.fori_loop(0, 8, member, 0)
    ld_cot.wait()
    for h in range(2):
        pro.s[h] = mm(m_t[h], cot[...]).astype(BF).reshape(YS, 128, W)
    pro.start()

    ld_fw.wait()
    wcat[0:256] = fw[0:256]
    wcat[256:1280] = mm(nodes[...], fw[256:512]).astype(BF)
    p_r[...] = mm(nodes[...], fw[512:768]).astype(BF)

    def edge_hot(t, c):
        for j in range(4):
            rows = slice(128 * j, 128 * j + 128)
            scol = column(snd[pl.ds(4 * t + j, 1), :]).astype(jnp.int16)
            rcol = column(rcv[pl.ds(4 * t + j, 1), :] - 128 * t)
            for b in range(12):
                oh[t, b, rows, :] = hot16(scol == lane16 + jnp.int16(128 * b))
            ohr[t, rows, :] = hot((rcol == lane) & (sub + 128 * j < count))
        return c

    lax.fori_loop(0, TILES, edge_hot, 0, unroll=2)
    pro.pair()
    ld_edges.wait()

    def edge_local(i, c):
        rows = pl.ds(pl.multiple_of(i * BIG, BIG), BIG)
        tiles = [i * (BIG // 512) + q for q in range(BIG // 512)]
        far = [jnp.concatenate([oh[t, b] for b in range(8)], axis=1) for t in tiles]
        near = [mm(ohr[t], p_r[pl.ds(pl.multiple_of(t * 128, 128), 128), :]) for t in tiles]
        joined = jnp.concatenate([edges[rows, :], jnp.concatenate(far, axis=0)], axis=1)
        work[rows, :] = mm(joined, wcat[0:1280]) + jnp.concatenate(near, axis=0)
        return c

    lax.fori_loop(0, 4096 // BIG, edge_local, 0)
    x_halo.wait_recv()
    wcat[1280:1792] = mm(hin[...].reshape(512, W), fw[256:512]).astype(BF)

    def edge_forward(i, c):
        rows = pl.ds(pl.multiple_of(i * BIG, BIG), BIG)
        tiles = [i * (BIG // 512) + q for q in range(BIG // 512)]
        far = [jnp.concatenate([oh[t, b] for b in range(8, 12)], axis=1) for t in tiles]
        a, gp = silu_parts(work[rows, :] + mm(jnp.concatenate(far, axis=0), wcat[1280:1792]))
        act[rows, :] = a
        gpr[rows, :] = gp
        y, rs = norm(mm(a, fw[768:1024]))
        yv[rows, :] = y.astype(BF)
        rsv[rows, :] = rs
        return c

    def edge_sum(t, c):
        back = []
        for j in range(4):
            rrow = rcv[pl.ds(4 * t + j, 1), :] - 128 * t
            back.append(hot((rrow == sub) & (lane + 128 * j < count)))
        rows = pl.ds(pl.multiple_of(t * 512, 512), 512)
        summed[pl.ds(pl.multiple_of(t * 128, 128), 128), :] = mm(
            jnp.concatenate(back, axis=1), yv[rows, :]).astype(BF)
        return c

    lax.fori_loop(0, 4096 // BIG, edge_forward, 0)
    lax.fori_loop(0, TILES, edge_sum, 0, unroll=TILES)

    a, gp = silu_parts(mm(nodes[...], fw[1024:1280]) + mm(summed[...], fw[1280:1536]))
    an[...] = a
    gn[...] = gp
    ynode, rs = norm(mm(a, fw[1536:1792]))
    yn[...] = ynode.astype(BF)
    rsn[...] = rs
    refined[...] = (nodes[...].astype(F32) + ynode).astype(BF)
    hin_t = p_r
    hin_t[0:512] = hin[...].reshape(512, W)

    res.s[1 - core] = (mm(m_t[1 - core], refined[...]) * 0.125).astype(BF).reshape(YS, 128, W)
    res.start()
    res.s[core] = (mm(m_t[core], refined[...]) * 0.125).astype(BF).reshape(YS, 128, W)
    res.pair()

    def edge_hot_back(t, c):
        for j in range(4):
            rows = slice(128 * j, 128 * j + 128)
            srow = jnp.broadcast_to(snd[pl.ds(4 * t + j, 1), :], (128, 128)).astype(jnp.int16)
            rrow = rcv[pl.ds(4 * t + j, 1), :] - 128 * t
            for b in range(12):
                oh[t, b, rows, :] = hot16(srow == sub16 + jnp.int16(128 * b))
            oh[t, 12, rows, :] = hot((rrow == sub) & (lane + 128 * j < count))
        return c

    def member_back(j, c):
        col = column(agg[pl.ds(j, 1), :])
        for b in range(8):
            m_t[j // 4, pl.ds(pl.multiple_of(lax.rem(j, 4) * 128, 128), 128), 128 * b:128 * b + 128] = hot(col == lane + 128 * b)
        return c

    ld_ce.wait()
    ld_cw.wait()
    cback = []
    for j in range(4):
        srow = csnd[pl.ds(4 * g + j, 1), :]
        rrow = crcv[pl.ds(4 * g + j, 1), :]
        scol = column(srow)
        rcol = column(rrow)
        for b in range(8):
            m_t[0, 128 * j:128 * j + 128, 128 * b:128 * b + 128] = hot(scol == lane + 128 * b)
        cx[128 * j:128 * j + 128, :] = hot(rcol == lane)
        cback.append(hot(rrow == sub))
    cback = jnp.concatenate(cback, axis=1)
    cwc[0:256] = cw[0:256]
    pg = pro.result().astype(BF).astype(F32)
    lax.fori_loop(0, 3, edge_hot_back, 0)
    turn(nodes, 0, 4)
    turn(summed, 0, 4)
    turn(an, 0, 4)
    turn(hin_t, 0, 2)
    cin = res.result().astype(BF)
    cinb[g] = cin
    x_cin.start()
    cwc[1280:1408] = mm(cin, cw[512:768]).astype(BF)
    lax.fori_loop(3, TILES, edge_hot_back, 0)
    x_cin.wait_recv()
    cwc[256:1280] = mm(cinb[...].reshape(1024, W), cw[256:512]).astype(BF)
    ca, cg = silu_parts(mm(jnp.concatenate([ce[...], m_t[0], cx[...]], axis=1), cwc[...]))
    cact[...] = ca
    cgp[...] = cg
    cyn, rs = norm(mm(ca, cw[768:1024]))
    cyn = cyn.astype(BF)
    cy[...] = cyn
    crs[...] = rs
    csum = mm(cback, cyn).astype(BF)
    cna, cng = silu_parts(mm(cin, cw[1024:1280]) + mm(csum, cw[1280:1536]))
    cny, cnrs = norm(mm(cna, cw[1536:1792]))
    coutb[g] = (cin.astype(F32) + cny).astype(BF)

    cndz = norm_back(pg, cny, cnrs)
    cndh = (mm_nt(cndz, cw[1536:1792]) * cng.astype(F32)).astype(BF)
    dcin_part = pg + mm_nt(cndh, cw[1024:1280])
    dcsum = mm_nt(cndh, cw[1280:1536]).astype(BF)
    cdz = norm_back(mm(cx[...], dcsum), cy[...].astype(F32), crs[...])
    cdh = (mm_nt(cdz, cw[768:1024]) * cgp[...].astype(F32)).astype(BF)

    def sender_sum(half):
        blocks = []
        for p in range(YS):
            at = 128 * (2 * p + half)
            blocks.append(jnp.concatenate(
                [hot(csnd[pl.ds(4 * g + j, 1), :] - at == sub) for j in range(4)], axis=1))
        sen.s[half] = mm(jnp.concatenate(blocks, axis=0), cdh).astype(BF).reshape(YS, 128, W)

    sender_sum(1 - core)
    sen.start()
    sender_sum(core)
    s_cr = mm(cback, cdh).astype(BF)
    sen.pair()
    put(early.s, halves, 0, mm_tn(ce[...], cdh))
    put(early.s, halves, 256, mm_tn(cact[...], cdz))
    put(early.s, halves, 512, mm_tn(cin, cndh))
    put(early.s, halves, 768, mm_tn(csum, cndh))
    put(early.s, halves, 1024, mm_tn(cna, cndz))
    put(middle.s, halves, 0, mm_tn(cin, s_cr))
    dcin_part = dcin_part + mm_nt(s_cr, cw[512:768])
    lax.fori_loop(0, 8, member_back, 0)
    turn(edges, 0, 8)
    s_tot = sen.result().astype(BF)
    dcinb[g] = (dcin_part + mm_nt(s_tot, cw[256:512])).astype(BF)
    x_dcin.start()
    put(early.s, halves, 1280, mm_tn(cin, s_tot))
    early.stage0()

    early.stage1()
    turn(edges, 2048, 8)
    turn(act, 0, 16)
    x_dcin.wait_recv()
    x_cout.start()
    rg[...] = (cot[...].astype(F32) + 0.125 * mm(m_t[...].reshape(1024, 1024), dcinb[...].reshape(1024, W))).astype(BF)

    dz = norm_back(rg[...].astype(F32), yn[...].astype(F32), rsn[...])
    dh = (mm_nt(dz, fw[1536:1792]) * gn[...].astype(F32)).astype(BF)
    dnp[...] = rg[...].astype(F32) + mm_nt(dh, fw[1024:1280])
    dsum = mm_nt(dh, fw[1280:1536]).astype(BF).astype(F32)
    dsm[...] = (dsum - jnp.mean(dsum, axis=-1, keepdims=True)).astype(BF)
    put(middle.s, halves, 256, mm_turned(nodes, 0, 4, dh))
    put(middle.s, halves, 512, mm_turned(summed, 0, 4, dh))
    put(middle.s, halves, 768, mm_turned(an, 0, 4, dz))
    middle.stage0()
    early.stage2()

    s_s[...] = jnp.zeros_like(s_s)
    g_ae[...] = jnp.zeros_like(g_ae)
    g_b[...] = jnp.zeros_like(g_b)

    def edge_backward(i):
        base = i * BIG
        rows = pl.ds(base, BIG)
        tiles = [i * (BIG // 512) + q for q in range(BIG // 512)]
        dmsg = jnp.concatenate([mm(ohr[t], dsm[128 * t:128 * t + 128, :]) for t in tiles], axis=0)
        dz = norm_back_centred(dmsg, yv[rows, :].astype(F32), rsv[rows, :])
        dh = (mm_nt(dz, fw[768:1024]) * gpr[rows, :].astype(F32)).astype(BF)
        gpr[rows, :] = dh
        g_b[...] += mm_turned(act, base, BIG // 256, dz)
        g_ae[...] += mm_turned(edges, base, BIG // 256, dh)

        def turned(t, b):
            return jnp.concatenate([oh[t, b, 128 * j:128 * j + 128, :] for j in range(4)], axis=1)

        for q in range(3):
            part = [jnp.concatenate([turned(t, 4 * q + b) for t in tiles], axis=1) for b in range(4)]
            s_s[512 * q:512 * q + 512, :] += mm(jnp.concatenate(part, axis=0), dh)
        for q, t in enumerate(tiles):
            s_r[128 * t:128 * t + 128, :] = mm(turned(t, 12), dh[512 * q:512 * q + 512]).astype(BF)

    for i in range(4096 // BIG):
        if i == 4096 // BIG // 2:
            early.stage3()
            middle.stage1()
        edge_backward(i)

    put(late.s, halves, 0, g_ae[...])
    put(late.s, halves, 256, g_b[...])
    ss = s_s[...].astype(BF)
    put(late.s, halves, 512, mm_turned(nodes, 0, 4, ss[0:1024]) + mm_turned(hin_t, 0, 2, ss[1024:1536]))
    put(late.s, halves, 768, mm_turned(nodes, 0, 4, s_r[...]))
    late.stage0()
    hret[...] = mm_nt(ss[1024:1536], fw[256:512]).astype(BF).reshape(16, 32, W)
    late.stage1()
    x_ret.start()
    middle.stage2()
    early.stage4()

    for i in range(4096 // BIG):
        rows = pl.ds(i * BIG, BIG)
        edge_grad[rows, :] = mm_nt(gpr[rows, :], fw[0:256]).astype(BF)
    st_edge = pltpu.make_async_copy(edge_grad, edge_grad_h, osem.at[1])
    st_edge.start()
    x_cout.wait_recv()
    fine_out[...] = (refined[...].astype(F32) + mm(m_t[...].reshape(1024, 1024), coutb[...].reshape(1024, W))).astype(BF)
    st_fine = pltpu.make_async_copy(fine_out, fine_out_h, osem.at[0])
    st_fine.start()
    own = dnp[...] + mm_nt(ss[0:1024], fw[256:512]) + mm_nt(s_r[...], fw[512:768])
    late.stage2()
    middle.stage3()
    x_ret.wait_recv()
    node_grad[...] = (own + mm_tn(ohh[...], hrin[...].reshape(512, W))).astype(BF)
    st_node = pltpu.make_async_copy(node_grad, node_grad_h, osem.at[2])
    st_node.start()
    late.stage3()
    early.finish()
    stores = [st_fine, st_edge, st_node]

    def store(ref, at):
        rows = ref.shape[0]
        copy = pltpu.make_async_copy(ref, grads_h.at[pl.ds(at, rows)], osem.at[len(stores)])
        copy.start()
        stores.append(copy)

    def store_blocks(ref, at):
        rows = ref.shape[-2]
        if len(ref.shape) == 4:
            for h in range(2):
                store_blocks(ref.at[h], at + h * DOM * rows)
        else:
            n = ref.shape[0]
            flat = staged.at[pl.ds(at, n * rows)]
            flat[...] = ref[...].reshape(n * rows, W)
            store(flat, at)

    store_blocks(early.o, 0)
    middle.stage4()
    late.stage4()
    middle.finish()
    store_blocks(middle.o, 1536)
    late.finish()
    store_blocks(late.o, 2560)
    for c in stores:
        c.wait()
    for x in links.all:
        x.wait_send()


def place(
    fine_h, node_h, edge_h, grads_h, fine_o, node_o, edge_o, fw_o, cw_o,
    fine, node, edge, grads, fwg, cwg, lsem, ssem,
):
    half = edge.shape[0] // 2
    parts = [(grads_h, grads, None), (fine_h, fine, fine_o), (node_h, node, node_o)]
    for i in range(2):
        rows = pl.ds(half * i, half)
        parts.append((edge_h.at[rows], edge.at[rows], edge_o.at[rows]))
    loads = [pltpu.make_async_copy(a, b, lsem.at[i]) for i, (a, b, c) in enumerate(parts)]
    moves = [pltpu.make_async_copy(b, c, ssem.at[i]) for i, (a, b, c) in enumerate(parts) if i > 0]
    for c in loads:
        c.start()
    loads[0].wait()

    def scaled(at, rows, scale):
        return grads[at:at + rows].astype(F32) * scale

    last = [pltpu.make_async_copy(cwg, cw_o, ssem.at[5]), pltpu.make_async_copy(fwg, fw_o, ssem.at[6])]
    cwg[0:256] = scaled(0, 256, COARSE_SCALE)
    cwg[256:768] = scaled(1280, 512, COARSE_SCALE)
    cwg[768:1792] = scaled(256, 1024, COARSE_SCALE)
    last[0].start()
    for c, m in zip(loads[1:], moves):
        c.wait()
        m.start()
    fwg[0:256] = scaled(2560, 256, FINE_SCALE)
    fwg[256:768] = scaled(3072, 512, FINE_SCALE)
    fwg[768:1024] = scaled(2816, 256, FINE_SCALE)
    fwg[1024:1792] = scaled(1792, 768, FINE_SCALE)
    last[1].start()
    for c in moves + last:
        c.wait()


def body(
    nodes, edges, senders, receivers, edge_count, halo_rows, aggregates,
    coarse_edges, coarse_senders, coarse_receivers, cotangent, fine_weights, coarse_weights,
):
    vm = pl.BlockSpec(memory_space=pltpu.VMEM)
    hbm = pl.BlockSpec(memory_space=pl.ANY)
    V = pltpu.VMEM
    scratch = [
        V((1024, W), BF),
        V((4096, W), BF),
        V((1024, W), BF),
        V((1792, W), BF),
        V((1792, W), BF),
        V((512, W), BF),
        V((16, 128), jnp.int32),
        V((8, 128), jnp.int32),
        V((512, 1024), BF),
        V((16, 32, W), BF),
        V((16, 32, W), BF),
        V((2, 512, 1024), BF),
        V((8, 13, 512, 128), BF),
        V((8, 512, 128), BF),
        V((1792, W), BF),
        V((1024, W), BF),
        V((4096, W), BF),
        V((4096, W), BF),
        V((4096, W), BF),
        V((4096, 1), F32),
        V((1024, W), BF),
        V((1024, W), BF),
        V((1024, W), BF),
        V((1024, W), BF),
        V((1024, 1), F32),
        V((1024, W), BF),
        V((8, 128, W), BF),
        V((512, 128), BF),
        V((1408, W), BF),
        V((512, W), BF),
        V((512, W), BF),
        V((512, W), BF),
        V((512, 1), F32),
        V((8, 128, W), BF),
        V((8, 128, W), BF),
        V((1024, W), BF),
        V((4096, W), F32),
        V((1024, W), BF),
        V((1024, W), BF),
        V((16, 32, W), BF),
        V((16, 32, W), BF),
        pltpu.SemaphoreType.DMA((256,)),
        pltpu.SemaphoreType.DMA((256,)),
        pltpu.SemaphoreType.DMA((6,)),
        pltpu.SemaphoreType.DMA((12,)),
    ]
    for _ in range(3):
        scratch += [V((2, YS, 128, W), BF), V((YS, 128, W), BF), V((YS, 128, W), BF), V((YS, 128, W), BF)]
    for rows in (48, 32, 32):
        scratch += [V((2, DOM, rows, W), BF), V((DOM, rows, W), BF), V((DOM, rows, W), BF),
                    V((DOM, rows, W), BF), V((YS, rows, W), BF), V((2, DOM, rows, W), BF)]
    shape = jax.ShapeDtypeStruct
    fine_out, node_grad, edge_grad, grads = pl.pallas_call(
        kernel,
        out_shape=(shape((1024, W), BF), shape((1024, W), BF), shape((4096, W), BF), shape((3584, W), BF)),
        in_specs=[hbm, hbm, vm, vm, pl.BlockSpec(memory_space=pltpu.SMEM), vm, vm,
                  hbm, vm, vm, hbm, hbm, hbm],
        out_specs=(hbm,) * 4,
        scratch_shapes=scratch,
        compiler_params=pltpu.CompilerParams(
            collective_id=0, has_side_effects=True, vmem_limit_bytes=64 * 1024 * 1024 - 65536
        ),
    )(
        nodes, edges, senders.reshape(32, 128), receivers.reshape(32, 128), edge_count,
        halo_rows.reshape(16, 32), aggregates.reshape(8, 128), coarse_edges,
        coarse_senders.reshape(32, 128), coarse_receivers.reshape(32, 128), cotangent,
        fine_weights, coarse_weights,
    )
    return pl.pallas_call(
        place,
        out_shape=(shape((1024, W), BF), shape((1024, W), BF), shape((4096, W), BF),
                   shape((1792, W), F32), shape((1792, W), F32)),
        in_specs=[hbm] * 4,
        out_specs=(hbm,) * 5,
        scratch_shapes=[V((1024, W), BF), V((1024, W), BF), V((4096, W), BF), V((3584, W), BF), V((1792, W), F32),
                        V((1792, W), F32), pltpu.SemaphoreType.DMA((5,)), pltpu.SemaphoreType.DMA((7,))],
        compiler_params=pltpu.CompilerParams(vmem_limit_bytes=62 * 1024 * 1024),
    )(fine_out, node_grad, edge_grad, grads)


def solution(mesh):
    both = ("dom", "grp")
    placed = (
        P(both, None), P(both, None), P(both), P(both), P(both), P(both, None, None), P(both),
        P("dom", None, None), P("dom", None), P("dom", None), P(both, None), P(), P(),
    )
    return jax.shard_map(
        body, mesh=mesh, in_specs=placed,
        out_specs=(P(both, None), P(both, None), P(both, None), P(), P()),
        check_vma=False,
    )
```

```python
import jax
import jax.numpy as jnp
from jax import lax
from jax.experimental import pallas as pl
from jax.experimental.pallas import tpu as pltpu
from jax.sharding import PartitionSpec as P

MESH = pl.DeviceIdType.MESH
BF = jnp.bfloat16
F32 = jnp.float32
W = 256
DOM = 16
GRP = 8
TILES = 8
YS = 4
BIG = 2048
FINE_SCALE = 524288 ** (-0.5)
COARSE_SCALE = 65536 ** (-0.5)


def mm(a, b):
    return jnp.dot(a, b, preferred_element_type=F32)


def mm_nt(a, b):
    return lax.dot_general(a, b, (((1,), (1,)), ((), ())), preferred_element_type=F32)


def mm_tn(a, b):
    return lax.dot_general(a, b, (((0,), (0,)), ((), ())), preferred_element_type=F32)


def iota(shape, axis):
    return lax.broadcasted_iota(jnp.int32, shape, axis)


def hot(mask):
    return jnp.where(mask, 1.0, 0.0).astype(BF)


def hot16(mask):
    return jnp.where(mask, jnp.ones(mask.shape, BF), jnp.zeros(mask.shape, BF))


def column(row):
    return jnp.broadcast_to(row, (128, 128)).T


def silu_parts(h):
    sig = 1.0 / (1.0 + jnp.exp(-h))
    active = h * sig
    return active.astype(BF), (sig * (1.0 + h - active)).astype(BF)


def norm(z):
    centre = z - jnp.mean(z, axis=-1, keepdims=True)
    rs = lax.rsqrt(jnp.mean(centre * centre, axis=-1, keepdims=True) + 1e-05)
    return centre * rs, rs


def norm_back(dy, y, rs):
    first = jnp.mean(dy, axis=-1, keepdims=True)
    second = jnp.mean(dy * y, axis=-1, keepdims=True)
    return (rs * (dy - first - y * second)).astype(BF)


def norm_back_centred(dy, y, rs):
    second = jnp.mean(dy * y, axis=-1, keepdims=True)
    return (rs * (dy - y * second)).astype(BF)


def turn(ref, rows, count):
    def step(i, c):
        block = pl.ds(pl.multiple_of(rows + 256 * i, 256), 256)
        ref[block, :] = ref[block, :].T
        return c

    lax.fori_loop(0, count, step, 0)


def mm_turned(ref, rows, count, b):
    left = [ref[rows + 256 * i:rows + 256 * i + 256, :] for i in range(count)]
    return mm(jnp.concatenate(left, axis=1), b)


class Links:
    def __init__(self, ssem, rsem):
        self.d, self.g = lax.axis_index("dom"), lax.axis_index("grp")
        self.y, self.core = self.g // 2, lax.rem(self.g, 2)
        self.ssem, self.rsem, self.used = ssem, rsem, 0
        self.all = []

    def exchange(self, kind, src, dst):
        x = Exchange(self, kind, src, dst, self.used)
        self.used += x.count
        self.all.append(x)
        return x


class Exchange:
    def __init__(self, at, kind, src, dst, off):
        self.at, self.kind, self.src, self.dst, self.off = at, kind, src, dst, off
        self.count = {"dom": DOM, "grp": GRP, "y": YS, "mate": 2}[kind]

    def copy(self, k):
        at = self.at
        if self.kind == "dom":
            p = lax.rem(at.d + k, DOM)
            device = {"dom": p}
        elif self.kind == "grp":
            p = lax.rem(at.g + k, GRP)
            device = {"grp": p}
        elif self.kind == "y":
            p = lax.rem(at.y + k, YS)
            device = {"grp": 2 * p + at.core}
        else:
            p = 1 - at.core
            device = {"grp": 2 * at.y + p}
        return pltpu.make_async_remote_copy(
            src_ref=self.src(p),
            dst_ref=self.dst(k),
            send_sem=self.at.ssem.at[self.off + k],
            recv_sem=self.at.rsem.at[self.off + k],
            device_id=device,
            device_id_type=MESH,
        )

    def each(self, act):
        def step(k, carry):
            act(self.copy(k))
            return carry

        for k in sorted(range(1, self.count), key=lambda k: abs(k - self.count // 2)):
            step(k, 0)

    def start(self):
        self.each(lambda c: c.start())

    def wait_recv(self):
        self.each(lambda c: c.wait_recv())

    def wait_send(self):
        self.each(lambda c: c.wait_send())


def total_of(first, blocks, which):
    total = first.astype(F32)
    for k in which:
        total = total + blocks[k].astype(F32)
    return total


class GroupSum:
    def __init__(self, links, s, m, t, r):
        self.links, self.s, self.m, self.t, self.r = links, s, m, t, r
        self.first = links.exchange("mate", lambda p: s.at[p], lambda k: m)
        self.second = links.exchange("y", lambda p: t.at[p], lambda k: r.at[k])

    def pair(self):
        self.first.wait_recv()
        self.t[...] = (self.s[self.links.core].astype(F32) + self.m[...].astype(F32)).astype(BF)
        self.second.start()

    def result(self):
        self.second.wait_recv()
        return total_of(self.t[self.links.y], self.r, range(1, YS))


class GroupGather:
    def __init__(self, links, b):
        self.links, self.b = links, b
        g, y, core = links.g, links.y, links.core
        self.mate = links.exchange("mate", lambda p: b.at[g], lambda k: b.at[g])
        self.far = links.exchange("y", lambda p: b.at[g], lambda k: b.at[g])
        self.passed = []
        for k in range(1, YS):
            p = 2 * lax.rem(y + YS - k, YS) + core
            self.passed.append(links.exchange("mate", lambda q, p=p: b.at[p], lambda q, p=p: b.at[p]))

    def start(self):
        self.far.start()
        self.mate.start()

    def wait_recv(self):
        for k in range(1, YS):
            self.far.copy(k).wait_recv()
            self.passed[k - 1].start()
        self.mate.wait_recv()
        for x in self.passed:
            x.wait_recv()


class AllSum:
    def __init__(self, links, s, m, t, r, v, o):
        self.links, self.s, self.m, self.t, self.r, self.v, self.o = links, s, m, t, r, v, o
        d, y, core = links.d, links.y, links.core
        self.x0 = links.exchange("mate", lambda p: s.at[p], lambda k: m)
        self.x1 = links.exchange("dom", lambda p: t.at[p], lambda k: r.at[k])
        self.x2 = links.exchange("y", lambda p: v.at[y], lambda k: v.at[y])
        self.x3 = links.exchange("dom", lambda p: o.at[core, d], lambda k: o.at[core, d])
        self.x4 = links.exchange("mate", lambda p: o.at[core], lambda k: o.at[core])

    def stage0(self):
        self.x0.start()

    def stage1(self):
        self.x0.wait_recv()
        self.t[...] = (self.s[self.links.core].astype(F32) + self.m[...].astype(F32)).astype(BF)
        self.x1.start()

    def stage2(self):
        self.x1.wait_recv()
        self.v[self.links.y] = total_of(self.t[self.links.d], self.r, range(1, DOM)).astype(BF)
        self.x2.start()

    def stage3(self):
        self.x2.wait_recv()
        self.o[self.links.core, self.links.d] = total_of(self.v[0], self.v, range(1, YS)).astype(BF)
        self.x3.start()

    def stage4(self):
        self.x3.wait_recv()
        self.x4.start()

    def finish(self):
        self.x4.wait_recv()


def put(ref, lead, at, value):
    value = value.astype(BF)
    rows, pos = ref.shape[-2], 0
    while pos < value.shape[0]:
        block, inside = (at + pos) // rows, (at + pos) % rows
        n = min(rows - inside, value.shape[0] - pos)
        ref[lead(block) + (slice(inside, inside + n), slice(None))] = value[pos:pos + n]
        pos += n


def halves(block):
    return (block // DOM, block % DOM)


def kernel(
    nodes_h, edges_h, snd, rcv, cnt, halo, agg, cedges_h, csnd, crcv, cot_h, fw_h, cw_h,
    fine_out_h, node_grad_h, edge_grad_h, grads_h, *s
):
    (nodes, edges, cot, fw, cw, ce,
     hpad, hr, ohh, outg, hin, m_t, oh, ohr, wcat, p_r, act, gpr, yv, rsv, summed,
     an, gn, yn, rsn, refined, cinb, cx, cwc, cact, cgp, cy, crs, coutb,
     dcinb, rg, work, dsm, s_r, hret, hrin, ssem, rsem, isem, osem) = s[:45]
    rest = list(s[45:])
    edge_grad, staged, fine_out, node_grad = yv, act, refined, rg
    s_s, dnp = work.at[0:1536], work.at[1536:2560]
    g_ae, g_b = work.at[2560:2816], work.at[2816:3072]

    def take(n):
        out = rest[:n]
        del rest[:n]
        return out

    links = Links(ssem, rsem)
    d, g, y, core = links.d, links.g, links.y, links.core
    count = cnt[0]

    loads = [
        pltpu.make_async_copy(src, dst, isem.at[i])
        for i, (src, dst) in enumerate((
            (nodes_h, nodes), (fw_h, fw), (cot_h, cot), (edges_h, edges), (cw_h, cw),
            (cedges_h.at[0, pl.ds(pl.multiple_of(g * 512, 512), 512)], ce),
        ))
    ]
    for c in loads:
        c.start()
    ld_nodes, ld_fw, ld_cot, ld_edges, ld_cw, ld_ce = loads
    barrier = pltpu.get_barrier_semaphore()

    def greet_dom(k, c):
        pl.semaphore_signal(barrier, inc=1, device_id={"dom": lax.rem(d + k, DOM)}, device_id_type=MESH)
        return c

    def greet_grp(k, c):
        pl.semaphore_signal(barrier, inc=1, device_id={"grp": lax.rem(g + k, GRP)}, device_id_type=MESH)
        return c

    lax.fori_loop(1, DOM, greet_dom, 0)
    lax.fori_loop(1, GRP, greet_grp, 0)

    x_halo = links.exchange("dom", lambda p: outg.at[p], lambda k: hin.at[d])
    x_ret = links.exchange("dom", lambda p: hret.at[p], lambda k: hrin.at[d])
    pro = GroupSum(links, *take(4))
    res = GroupSum(links, *take(4))
    sen = GroupSum(links, *take(4))
    x_cin = GroupGather(links, cinb)
    x_cout = GroupGather(links, coutb)
    x_dcin = GroupGather(links, dcinb)
    early = AllSum(links, *take(6))
    middle = AllSum(links, *take(6))
    late = AllSum(links, *take(6))

    lane = iota((128, 128), 1)
    sub = iota((128, 128), 0)
    lane16 = lane.astype(jnp.int16)
    sub16 = sub.astype(jnp.int16)

    hpad[...] = jnp.zeros_like(hpad)
    hpad[:, 0:32] = halo[...]
    padded = hpad[...]
    rolled = [padded] + [pltpu.roll(padded, 32 * i, 1) for i in range(1, 4)]
    for j in range(4):
        row = rolled[0][4 * j:4 * j + 1]
        for i in range(1, 4):
            row = row + rolled[i][4 * j + i:4 * j + i + 1]
        hr[j:j + 1, :] = row
        col = column(row)
        for b in range(8):
            ohh[128 * j:128 * j + 128, 128 * b:128 * b + 128] = hot(col == lane + 128 * b)
    hin[d] = jnp.zeros((32, W), BF)
    hrin[d] = jnp.zeros((32, W), BF)
    ld_nodes.wait()
    outg[...] = mm(ohh[...], nodes[...]).astype(BF).reshape(16, 32, W)
    pl.semaphore_wait(barrier, DOM + GRP - 2)
    x_halo.start()

    def member(j, c):
        row = agg[pl.ds(j, 1), :]
        at = pl.multiple_of(j * 128, 128)
        for b in range(8):
            m_t[b % 2, 128 * (b // 2):128 * (b // 2) + 128, pl.ds(at, 128)] = hot(sub + 128 * b == row)
        return c

    lax.fori_loop(0, 8, member, 0)
    ld_cot.wait()
    for h in range(2):
        pro.s[h] = mm(m_t[h], cot[...]).astype(BF).reshape(YS, 128, W)
    pro.first.start()

    ld_fw.wait()
    wcat[0:256] = fw[0:256]
    wcat[256:1280] = mm(nodes[...], fw[256:512]).astype(BF)
    p_r[...] = mm(nodes[...], fw[512:768]).astype(BF)

    def edge_hot(t, c):
        for j in range(4):
            rows = slice(128 * j, 128 * j + 128)
            scol = column(snd[pl.ds(4 * t + j, 1), :]).astype(jnp.int16)
            rcol = column(rcv[pl.ds(4 * t + j, 1), :] - 128 * t)
            for b in range(12):
                oh[t, b, rows, :] = hot16(scol == lane16 + jnp.int16(128 * b))
            ohr[t, rows, :] = hot((rcol == lane) & (sub + 128 * j < count))
        return c

    lax.fori_loop(0, TILES, edge_hot, 0, unroll=2)
    pro.pair()
    ld_edges.wait()

    def edge_local(i, c):
        rows = pl.ds(0, 4096)
        tiles = range(TILES)
        far = [jnp.concatenate([oh[t, b] for b in range(8)], axis=1) for t in tiles]
        near = [mm(ohr[t], p_r[pl.ds(pl.multiple_of(t * 128, 128), 128), :]) for t in tiles]
        joined = jnp.concatenate([edges[rows, :], jnp.concatenate(far, axis=0)], axis=1)
        work[rows, :] = mm(joined, wcat[0:1280]) + jnp.concatenate(near, axis=0)
        return c

    edge_local(0, 0)
    x_halo.wait_recv()
    wcat[1280:1792] = mm(hin[...].reshape(512, W), fw[256:512]).astype(BF)

    def edge_forward(i, c):
        rows = pl.ds(pl.multiple_of(i * BIG, BIG), BIG)
        tiles = [i * (BIG // 512) + q for q in range(BIG // 512)]
        far = [jnp.concatenate([oh[t, b] for b in range(8, 12)], axis=1) for t in tiles]
        a, gp = silu_parts(work[rows, :] + mm(jnp.concatenate(far, axis=0), wcat[1280:1792]))
        act[rows, :] = a
        gpr[rows, :] = gp
        y, rs = norm(mm(a, fw[768:1024]))
        yv[rows, :] = y.astype(BF)
        rsv[rows, :] = rs
        return c

    def edge_sum(t, c):
        back = []
        for j in range(4):
            rrow = rcv[pl.ds(4 * t + j, 1), :] - 128 * t
            back.append(hot((rrow == sub) & (lane + 128 * j < count)))
        rows = pl.ds(pl.multiple_of(t * 512, 512), 512)
        summed[pl.ds(pl.multiple_of(t * 128, 128), 128), :] = mm(
            jnp.concatenate(back, axis=1), yv[rows, :]).astype(BF)
        return c

    lax.fori_loop(0, 4096 // BIG, edge_forward, 0)
    lax.fori_loop(0, TILES, edge_sum, 0, unroll=TILES)

    a, gp = silu_parts(mm(nodes[...], fw[1024:1280]) + mm(summed[...], fw[1280:1536]))
    an[...] = a
    gn[...] = gp
    ynode, rs = norm(mm(a, fw[1536:1792]))
    yn[...] = ynode.astype(BF)
    rsn[...] = rs
    refined[...] = (nodes[...].astype(F32) + ynode).astype(BF)
    hin_t = p_r
    hin_t[0:512] = hin[...].reshape(512, W)

    res.s[1 - core] = (mm(m_t[1 - core], refined[...]) * 0.125).astype(BF).reshape(YS, 128, W)
    res.first.start()
    res.s[core] = (mm(m_t[core], refined[...]) * 0.125).astype(BF).reshape(YS, 128, W)
    res.pair()

    def edge_hot_back(t, c):
        for j in range(4):
            rows = slice(128 * j, 128 * j + 128)
            srow = jnp.broadcast_to(snd[pl.ds(4 * t + j, 1), :], (128, 128)).astype(jnp.int16)
            rrow = rcv[pl.ds(4 * t + j, 1), :] - 128 * t
            for b in range(12):
                oh[t, b, rows, :] = hot16(srow == sub16 + jnp.int16(128 * b))
            oh[t, 12, rows, :] = hot((rrow == sub) & (lane + 128 * j < count))
        return c

    def member_back(j, c):
        col = column(agg[pl.ds(j, 1), :])
        for b in range(8):
            m_t[j // 4, pl.ds(pl.multiple_of(lax.rem(j, 4) * 128, 128), 128), 128 * b:128 * b + 128] = hot(col == lane + 128 * b)
        return c

    ld_ce.wait()
    ld_cw.wait()
    cback = []
    for j in range(4):
        srow = csnd[pl.ds(4 * g + j, 1), :]
        rrow = crcv[pl.ds(4 * g + j, 1), :]
        scol = column(srow)
        rcol = column(rrow)
        for b in range(8):
            m_t[0, 128 * j:128 * j + 128, 128 * b:128 * b + 128] = hot(scol == lane + 128 * b)
        cx[128 * j:128 * j + 128, :] = hot(rcol == lane)
        cback.append(hot(rrow == sub))
    cback = jnp.concatenate(cback, axis=1)
    cwc[0:256] = cw[0:256]
    pg = pro.result().astype(BF).astype(F32)
    lax.fori_loop(0, 3, edge_hot_back, 0)
    turn(nodes, 0, 4)
    turn(summed, 0, 4)
    turn(an, 0, 4)
    turn(hin_t, 0, 2)
    cin = res.result().astype(BF)
    cinb[g] = cin
    x_cin.start()
    cwc[1280:1408] = mm(cin, cw[512:768]).astype(BF)
    lax.fori_loop(3, TILES, edge_hot_back, 0)
    x_cin.wait_recv()
    cwc[256:1280] = mm(cinb[...].reshape(1024, W), cw[256:512]).astype(BF)
    ca, cg = silu_parts(mm(jnp.concatenate([ce[...], m_t[0], cx[...]], axis=1), cwc[...]))
    cact[...] = ca
    cgp[...] = cg
    cyn, rs = norm(mm(ca, cw[768:1024]))
    cyn = cyn.astype(BF)
    cy[...] = cyn
    crs[...] = rs
    csum = mm(cback, cyn).astype(BF)
    cna, cng = silu_parts(mm(cin, cw[1024:1280]) + mm(csum, cw[1280:1536]))
    cny, cnrs = norm(mm(cna, cw[1536:1792]))
    coutb[g] = (cin.astype(F32) + cny).astype(BF)

    cndz = norm_back(pg, cny, cnrs)
    cndh = (mm_nt(cndz, cw[1536:1792]) * cng.astype(F32)).astype(BF)
    dcin_part = pg + mm_nt(cndh, cw[1024:1280])
    dcsum = mm_nt(cndh, cw[1280:1536]).astype(BF)
    cdz = norm_back(mm(cx[...], dcsum), cy[...].astype(F32), crs[...])
    cdh = (mm_nt(cdz, cw[768:1024]) * cgp[...].astype(F32)).astype(BF)

    def sender_sum(half):
        blocks = []
        for p in range(YS):
            at = 128 * (2 * p + half)
            blocks.append(jnp.concatenate(
                [hot(csnd[pl.ds(4 * g + j, 1), :] - at == sub) for j in range(4)], axis=1))
        sen.s[half] = mm(jnp.concatenate(blocks, axis=0), cdh).astype(BF).reshape(YS, 128, W)

    sender_sum(1 - core)
    sen.first.start()
    sender_sum(core)
    s_cr = mm(cback, cdh).astype(BF)
    sen.pair()
    put(early.s, halves, 0, mm_tn(ce[...], cdh))
    put(early.s, halves, 256, mm_tn(cact[...], cdz))
    put(early.s, halves, 512, mm_tn(cin, cndh))
    put(early.s, halves, 768, mm_tn(csum, cndh))
    put(early.s, halves, 1024, mm_tn(cna, cndz))
    put(middle.s, halves, 0, mm_tn(cin, s_cr))
    dcin_part = dcin_part + mm_nt(s_cr, cw[512:768])
    lax.fori_loop(0, 8, member_back, 0)
    turn(edges, 0, 8)
    s_tot = sen.result().astype(BF)
    dcinb[g] = (dcin_part + mm_nt(s_tot, cw[256:512])).astype(BF)
    x_dcin.start()
    put(early.s, halves, 1280, mm_tn(cin, s_tot))
    early.stage0()

    early.stage1()
    turn(edges, 2048, 8)
    turn(act, 0, 16)
    x_dcin.wait_recv()
    x_cout.start()
    rg[...] = (cot[...].astype(F32) + 0.125 * mm(m_t[...].reshape(1024, 1024), dcinb[...].reshape(1024, W))).astype(BF)

    dz = norm_back(rg[...].astype(F32), yn[...].astype(F32), rsn[...])
    dh = (mm_nt(dz, fw[1536:1792]) * gn[...].astype(F32)).astype(BF)
    dnp[...] = rg[...].astype(F32) + mm_nt(dh, fw[1024:1280])
    dsum = mm_nt(dh, fw[1280:1536]).astype(BF).astype(F32)
    dsm[...] = (dsum - jnp.mean(dsum, axis=-1, keepdims=True)).astype(BF)
    put(middle.s, halves, 256, mm_turned(nodes, 0, 4, dh))
    put(middle.s, halves, 512, mm_turned(summed, 0, 4, dh))
    put(middle.s, halves, 768, mm_turned(an, 0, 4, dz))
    middle.stage0()
    early.stage2()

    s_s[...] = jnp.zeros_like(s_s)
    g_ae[...] = jnp.zeros_like(g_ae)
    g_b[...] = jnp.zeros_like(g_b)

    def edge_backward(i):
        base = i * BIG
        rows = pl.ds(base, BIG)
        tiles = [i * (BIG // 512) + q for q in range(BIG // 512)]
        dmsg = jnp.concatenate([mm(ohr[t], dsm[128 * t:128 * t + 128, :]) for t in tiles], axis=0)
        dz = norm_back_centred(dmsg, yv[rows, :].astype(F32), rsv[rows, :])
        dh = (mm_nt(dz, fw[768:1024]) * gpr[rows, :].astype(F32)).astype(BF)
        gpr[rows, :] = dh
        g_b[...] += mm_turned(act, base, BIG // 256, dz)
        g_ae[...] += mm_turned(edges, base, BIG // 256, dh)

        def turned(t, b):
            return jnp.concatenate([oh[t, b, 128 * j:128 * j + 128, :] for j in range(4)], axis=1)

        for q in range(3):
            part = [jnp.concatenate([turned(t, 4 * q + b) for t in tiles], axis=1) for b in range(4)]
            s_s[512 * q:512 * q + 512, :] += mm(jnp.concatenate(part, axis=0), dh)
        for q, t in enumerate(tiles):
            s_r[128 * t:128 * t + 128, :] = mm(turned(t, 12), dh[512 * q:512 * q + 512]).astype(BF)

    for i in range(4096 // BIG):
        if i == 4096 // BIG // 2:
            early.stage3()
            middle.stage1()
        edge_backward(i)

    put(late.s, halves, 0, g_ae[...])
    put(late.s, halves, 256, g_b[...])
    ss = s_s[...].astype(BF)
    put(late.s, halves, 512, mm_turned(nodes, 0, 4, ss[0:1024]) + mm_turned(hin_t, 0, 2, ss[1024:1536]))
    put(late.s, halves, 768, mm_turned(nodes, 0, 4, s_r[...]))
    late.stage0()
    hret[...] = mm_nt(ss[1024:1536], fw[256:512]).astype(BF).reshape(16, 32, W)
    late.stage1()
    x_ret.start()
    middle.stage2()
    early.stage4()

    for i in range(4096 // BIG):
        rows = pl.ds(i * BIG, BIG)
        edge_grad[rows, :] = mm_nt(gpr[rows, :], fw[0:256]).astype(BF)
    st_edge = pltpu.make_async_copy(edge_grad, edge_grad_h, osem.at[1])
    st_edge.start()
    x_cout.wait_recv()
    fine_out[...] = (refined[...].astype(F32) + mm(m_t[...].reshape(1024, 1024), coutb[...].reshape(1024, W))).astype(BF)
    st_fine = pltpu.make_async_copy(fine_out, fine_out_h, osem.at[0])
    st_fine.start()
    own = dnp[...] + mm_nt(ss[0:1024], fw[256:512]) + mm_nt(s_r[...], fw[512:768])
    late.stage2()
    middle.stage3()
    x_ret.wait_recv()
    node_grad[...] = (own + mm_tn(ohh[...], hrin[...].reshape(512, W))).astype(BF)
    st_node = pltpu.make_async_copy(node_grad, node_grad_h, osem.at[2])
    st_node.start()
    late.stage3()
    early.finish()
    stores = [st_fine, st_edge, st_node]

    def store(ref, at):
        rows = ref.shape[0]
        copy = pltpu.make_async_copy(ref, grads_h.at[pl.ds(at, rows)], osem.at[len(stores)])
        copy.start()
        stores.append(copy)

    def store_blocks(ref, at):
        rows = ref.shape[-2]
        if len(ref.shape) == 4:
            for h in range(2):
                store_blocks(ref.at[h], at + h * DOM * rows)
        else:
            n = ref.shape[0]
            flat = staged.at[pl.ds(at, n * rows)]
            flat[...] = ref[...].reshape(n * rows, W)
            store(flat, at)

    store_blocks(early.o, 0)
    middle.stage4()
    late.stage4()
    middle.finish()
    store_blocks(middle.o, 1536)
    late.finish()
    store_blocks(late.o, 2560)
    for c in stores:
        c.wait()
    for x in links.all:
        x.wait_send()


def place(
    fine_h, node_h, edge_h, grads_h, fine_o, node_o, edge_o, fw_o, cw_o,
    fine, node, edge, grads, fwg, cwg, lsem, ssem,
):
    half = edge.shape[0] // 2
    parts = [(grads_h, grads, None), (fine_h, fine, fine_o), (node_h, node, node_o)]
    for i in range(2):
        rows = pl.ds(half * i, half)
        parts.append((edge_h.at[rows], edge.at[rows], edge_o.at[rows]))
    loads = [pltpu.make_async_copy(a, b, lsem.at[i]) for i, (a, b, c) in enumerate(parts)]
    moves = [pltpu.make_async_copy(b, c, ssem.at[i]) for i, (a, b, c) in enumerate(parts) if i > 0]
    for c in loads:
        c.start()
    for c, m in zip(loads[1:], moves):
        c.wait()
        m.start()
    loads[0].wait()

    def scaled(at, rows, scale):
        return grads[at:at + rows].astype(F32) * scale

    cwg[0:256] = scaled(0, 256, COARSE_SCALE)
    cwg[256:768] = scaled(1280, 512, COARSE_SCALE)
    cwg[768:1792] = scaled(256, 1024, COARSE_SCALE)
    fwg[0:256] = scaled(2560, 256, FINE_SCALE)
    fwg[256:768] = scaled(3072, 512, FINE_SCALE)
    fwg[768:1024] = scaled(2816, 256, FINE_SCALE)
    fwg[1024:1792] = scaled(1792, 768, FINE_SCALE)
    last = [pltpu.make_async_copy(fwg, fw_o, ssem.at[5]), pltpu.make_async_copy(cwg, cw_o, ssem.at[6])]
    for c in last:
        c.start()
    for c in moves + last:
        c.wait()


def body(
    nodes, edges, senders, receivers, edge_count, halo_rows, aggregates,
    coarse_edges, coarse_senders, coarse_receivers, cotangent, fine_weights, coarse_weights,
):
    vm = pl.BlockSpec(memory_space=pltpu.VMEM)
    hbm = pl.BlockSpec(memory_space=pl.ANY)
    V = pltpu.VMEM
    scratch = [
        V((1024, W), BF),
        V((4096, W), BF),
        V((1024, W), BF),
        V((1792, W), BF),
        V((1792, W), BF),
        V((512, W), BF),
        V((16, 128), jnp.int32),
        V((8, 128), jnp.int32),
        V((512, 1024), BF),
        V((16, 32, W), BF),
        V((16, 32, W), BF),
        V((2, 512, 1024), BF),
        V((8, 13, 512, 128), BF),
        V((8, 512, 128), BF),
        V((1792, W), BF),
        V((1024, W), BF),
        V((4096, W), BF),
        V((4096, W), BF),
        V((4096, W), BF),
        V((4096, 1), F32),
        V((1024, W), BF),
        V((1024, W), BF),
        V((1024, W), BF),
        V((1024, W), BF),
        V((1024, 1), F32),
        V((1024, W), BF),
        V((8, 128, W), BF),
        V((512, 128), BF),
        V((1408, W), BF),
        V((512, W), BF),
        V((512, W), BF),
        V((512, W), BF),
        V((512, 1), F32),
        V((8, 128, W), BF),
        V((8, 128, W), BF),
        V((1024, W), BF),
        V((4096, W), F32),
        V((1024, W), BF),
        V((1024, W), BF),
        V((16, 32, W), BF),
        V((16, 32, W), BF),
        pltpu.SemaphoreType.DMA((256,)),
        pltpu.SemaphoreType.DMA((256,)),
        pltpu.SemaphoreType.DMA((6,)),
        pltpu.SemaphoreType.DMA((12,)),
    ]
    for _ in range(3):
        scratch += [V((2, YS, 128, W), BF), V((YS, 128, W), BF), V((YS, 128, W), BF), V((YS, 128, W), BF)]
    for rows in (48, 32, 32):
        scratch += [V((2, DOM, rows, W), BF), V((DOM, rows, W), BF), V((DOM, rows, W), BF),
                    V((DOM, rows, W), BF), V((YS, rows, W), BF), V((2, DOM, rows, W), BF)]
    shape = jax.ShapeDtypeStruct
    fine_out, node_grad, edge_grad, grads = pl.pallas_call(
        kernel,
        out_shape=(shape((1024, W), BF), shape((1024, W), BF), shape((4096, W), BF), shape((3584, W), BF)),
        in_specs=[hbm, hbm, vm, vm, pl.BlockSpec(memory_space=pltpu.SMEM), vm, vm,
                  hbm, vm, vm, hbm, hbm, hbm],
        out_specs=(hbm,) * 4,
        scratch_shapes=scratch,
        compiler_params=pltpu.CompilerParams(
            collective_id=0, has_side_effects=True, vmem_limit_bytes=64 * 1024 * 1024 - 65536
        ),
    )(
        nodes, edges, senders.reshape(32, 128), receivers.reshape(32, 128), edge_count,
        halo_rows.reshape(16, 32), aggregates.reshape(8, 128), coarse_edges,
        coarse_senders.reshape(32, 128), coarse_receivers.reshape(32, 128), cotangent,
        fine_weights, coarse_weights,
    )
    return pl.pallas_call(
        place,
        out_shape=(shape((1024, W), BF), shape((1024, W), BF), shape((4096, W), BF),
                   shape((1792, W), F32), shape((1792, W), F32)),
        in_specs=[hbm] * 4,
        out_specs=(hbm,) * 5,
        scratch_shapes=[V((1024, W), BF), V((1024, W), BF), V((4096, W), BF), V((3584, W), BF), V((1792, W), F32),
                        V((1792, W), F32), pltpu.SemaphoreType.DMA((5,)), pltpu.SemaphoreType.DMA((7,))],
        compiler_params=pltpu.CompilerParams(vmem_limit_bytes=62 * 1024 * 1024),
    )(fine_out, node_grad, edge_grad, grads)


def solution(mesh):
    both = ("dom", "grp")
    placed = (
        P(both, None), P(both, None), P(both), P(both), P(both), P(both, None, None), P(both),
        P("dom", None, None), P("dom", None), P("dom", None), P(both, None), P(), P(),
    )
    return jax.shard_map(
        body, mesh=mesh, in_specs=placed,
        out_specs=(P(both, None), P(both, None), P(both, None), P(), P()),
        check_vma=False,
    )
```
